512 devices in a mesh: gx: 64 (over y, z_hi, x), gy: 8 (over z_lo, core).
Axes of the slice: x: 4, y: 4, z: 16 (z_hi: 4, z_lo: 4; z = z_hi * 4 + z_lo), core: 2. Of those that a mesh axis runs over, the one named last changes fastest.
Arguments:
- field: float32 [20, 256, 256, 256], P(None, 'gx', 'gy'), may hold values from -6 to 6
- spectral_weight: bfloat16 [64, 64, 32, 2, 20, 20], P(None, 'gx', 'gy'), may hold values from -6 to 6
- point_weight: float32 [20, 20], replicated, may hold values from -1.25 to 1.25
- point_bias: float32 [20], replicated, may hold values from -4 to 4
Outputs:
- mixed_field: bfloat16 [20, 256, 256, 256], P(None, 'gx', 'gy')
The draws below stay inside these ranges and needn't reach their ends.
All inputs are finite; a program needn't handle non-finite values.
Results may differ from the reference program's by a relative error of at most 0.009.
Values may be sent and summed in bfloat16 or wider, within the bound.
No kernel may reach another device: no remote copies, remote signals or barrier semaphores. Data moves between devices by JAX's collectives and lax.ppermute only.
A program may use at most 64 MiB of HBM per device.

```python
import math
import jax
import jax.numpy as jnp
from jax import lax

C = 20
NX = 256
NY = 256
NZ = 256
KX = 64
KY = 64
KZ = 32


def shard_levels(key, extent, pieces, least, high):
    def one(dim, blocks):
        draws = jax.random.uniform(jax.random.fold_in(jax.random.fold_in(key, 6), dim), (blocks,), jnp.float32, least / len(pieces), high / len(pieces))
        return jnp.repeat(jnp.exp(draws), extent[dim] // blocks).reshape((-1,) + (1,) * (len(extent) - dim - 1))

    loudness = one(*pieces[0])
    for cut in pieces[1:]:
        loudness = loudness * one(*cut)
    return loudness


def bell_draw(key, shape, spread, most, cuts=(), kind=jnp.bfloat16):
    array = spread * jax.random.normal(key, shape, jnp.float32)
    if cuts:
        array = array * shard_levels(key, shape, cuts, -0.22, 0.18)
    return jnp.clip(array, -most, most).astype(kind)


def setup_inputs(seed: int = 0) -> dict:
    key_list = jax.random.split(jax.random.key(seed), 5)
    return {
        "field": bell_draw(key_list[0], (C, NX, NY, NZ), 1.0, 6.0, ((1, 64), (2, 8)), jnp.float32),
        "spectral_weight": bell_draw(key_list[1], (KX, KY, KZ, 2, C, C), 1.0, 6.0, ((1, 64), (2, 8))),
        "point_weight": bell_draw(key_list[2], (C, C), C ** -0.5, 1.25, (), jnp.float32),
        "point_bias": bell_draw(key_list[3], (C,), 1.0, 4.0, (), jnp.float32),
    }


def kept_freqs(number):
    index = jnp.arange(number, dtype=jnp.int32)
    return jnp.where(index < number // 2, index, index - number)

def phase_angles(first_pos, second_pos, length):
    product = jnp.mod(first_pos[:, None] * second_pos[None, :], length)
    return 2.0 * jnp.pi / length * product.astype(jnp.float32)

def forward_table(length, number):
    theta = phase_angles(jnp.arange(length, dtype=jnp.int32), kept_freqs(number), length)
    scale = 1.0 / math.sqrt(length)
    cosine = jnp.cos(theta) * scale
    sine = jnp.sin(theta) * scale
    return jnp.stack([jnp.stack([cosine, -sine], 1), jnp.stack([sine, cosine], 1)], 0)

def inverse_table(length, number):
    theta = phase_angles(kept_freqs(number), jnp.arange(length, dtype=jnp.int32), length)
    scale = 1.0 / math.sqrt(length)
    cosine = jnp.cos(theta) * scale
    sine = jnp.sin(theta) * scale
    return jnp.stack([jnp.stack([cosine, sine], 1), jnp.stack([-sine, cosine], 1)], 0)

def z_forward_table(length, number):
    theta = phase_angles(jnp.arange(length, dtype=jnp.int32), jnp.arange(number, dtype=jnp.int32), length)
    scale = 1.0 / math.sqrt(length)
    return jnp.concatenate([jnp.cos(theta), -jnp.sin(theta)], 1) * scale

def z_inverse_table(length, number):
    theta = phase_angles(jnp.arange(number, dtype=jnp.int32), jnp.arange(length, dtype=jnp.int32), length)
    scale = 1.0 / math.sqrt(length)
    factor = jnp.where(jnp.arange(number) == 0, 1.0, 2.0)[:, None] * scale
    return jnp.stack([factor * jnp.cos(theta), -factor * jnp.sin(theta)], 0)

def as_wide(table):
    return table.astype(jnp.bfloat16).astype(jnp.float32)

def reference(field, spectral_weight, point_weight, point_bias):
    z_table = z_forward_table(NZ, KZ)

    def z_step(channel):
        return jnp.einsum('xyz,zk->xyk', channel, z_table, precision=lax.Precision.HIGHEST).astype(jnp.bfloat16)
    z_modes = lax.map(z_step, field).reshape(C, NX, NY, 2, KZ)
    y_modes = jnp.einsum('cxypz,pyqk->cxkqz', z_modes.astype(jnp.float32), as_wide(forward_table(NY, KY))).astype(jnp.bfloat16)
    x_modes = jnp.einsum('cxypz,pxqk->ykzqc', y_modes.astype(jnp.float32), as_wide(forward_table(NX, KX))).astype(jnp.bfloat16)
    weight = spectral_weight.astype(jnp.float32)
    real_w = weight[:, :, :, 0]
    imag_w = weight[:, :, :, 1]
    real_a = x_modes[:, :, :, 0].astype(jnp.float32)
    imag_a = x_modes[:, :, :, 1].astype(jnp.float32)
    real_o = jnp.einsum('ykzc,kyzco->ykzo', real_a, real_w) - jnp.einsum('ykzc,kyzco->ykzo', imag_a, imag_w)
    imag_o = jnp.einsum('ykzc,kyzco->ykzo', real_a, imag_w) + jnp.einsum('ykzc,kyzco->ykzo', imag_a, real_w)
    spectrum = jnp.stack([real_o, imag_o], 3).astype(jnp.bfloat16)
    x_back = jnp.einsum('ykzpc,pkqx->cxyqz', spectrum.astype(jnp.float32), as_wide(inverse_table(NX, KX))).astype(jnp.bfloat16)
    y_back = jnp.einsum('cxkpz,pkqy->cxyqz', x_back.astype(jnp.float32), as_wide(inverse_table(NY, KY))).astype(jnp.bfloat16)
    z_inverse = as_wide(z_inverse_table(NZ, KZ))

    def out_step(items):
        channel_modes, column, shift = items
        spectral = jnp.einsum('xypk,pkz->xyz', channel_modes.astype(jnp.float32), z_inverse)
        pointwise = jnp.einsum('cxyz,c->xyz', field, column, precision=lax.Precision.HIGHEST)
        return jax.nn.gelu(spectral + pointwise + shift).astype(jnp.bfloat16)
    return lax.map(out_step, (y_back, point_weight.T, point_bias))
```

```python
import functools
import math

import jax
import jax.numpy as jnp
import numpy as np
from jax import lax
from jax.experimental import pallas as pl
from jax.experimental.pallas import tpu as pltpu
from jax.sharding import PartitionSpec as P

C = 20
NX = 256
NY = 256
NZ = 256
KX = 64
KY = 64
KZ = 32
F32 = jnp.float32
BF16 = jnp.bfloat16
MIB = 1 << 20
CHUNK = 4
LANES = 128


def kept_freqs(number):
    index = np.arange(number)
    return np.where(index < number // 2, index, index - number)


def waves(first_pos, second_pos, length):
    theta = 2.0 * np.pi / length * np.mod(np.multiply.outer(first_pos, second_pos), length)
    return np.cos(theta), np.sin(theta)


def z_table(gy, forward):
    shape = (2 * KZ, NZ)
    row = lax.broadcasted_iota(jnp.int32, shape, 0)
    cell = lax.broadcasted_iota(jnp.int32, shape, 1)
    own = KZ // gy
    mode = row // (2 * own) * own + row % own
    imaginary = row // own % 2 == 1
    turn = jnp.where(imaginary, NZ // 4, 0)
    angle = ((mode * cell + turn) % NZ).astype(F32) * (2.0 * math.pi / NZ)
    scale = 1.0 / math.sqrt(NZ)
    if not forward:
        scale = jnp.where(mode == 0, scale, 2.0 * scale)
    return (jnp.cos(angle) * scale).astype(BF16)


def y_waves(gy, xl, order):
    both = np.stack(waves(kept_freqs(KY), np.arange(NY), NY))[order] / math.sqrt(NY)
    both = both.reshape(2, KY, gy, NY // gy)
    table = np.einsum("tksy,ab->tsakby", both, np.eye(xl))
    return table.reshape(2, gy, xl * KY, xl * (NY // gy)).astype(jnp.bfloat16)


def x_pair(gx, xl, forward):
    cosine, sine = waves(kept_freqs(KX), np.arange(NX), NX)
    sign = 1.0 if forward else -1.0
    pair = np.stack([np.stack([cosine, -sign * sine]), np.stack([sign * sine, cosine])])
    if not forward:
        pair = pair.swapaxes(0, 1)
    pair = pair.reshape(2, 2, KX, gx, xl) / math.sqrt(NX)
    return pair.transpose(4, 3, 0, 1, 2).reshape(xl, 2 * gx, 2 * KX).astype(jnp.bfloat16)


def dot(a, b, ca, cb):
    return lax.dot_general(a, b, (((ca,), (cb,)), ((), ())), preferred_element_type=F32)


def vmem():
    return pl.BlockSpec(memory_space=pltpu.VMEM)


def hbm():
    return pl.BlockSpec(memory_space=pltpu.HBM)


def wide(ref, *index):
    *outer, last = index
    return jnp.concatenate([ref[(*outer, last)], ref[(*outer, last + 1)]], axis=1)


def rotated(gx, gy):
    step = gx // gy
    return [[(j + step * g) % gx * gy + g for j in range(gx)] for g in range(gy)]


def turn(cells, gx, gy, back):
    shift = 2 * (gx // gy) * lax.axis_index("gy")
    if not back:
        shift = lax.rem(2 * gx - shift, 2 * gx)
    return pltpu.roll(cells, shift, 0)


def z_forward_kernel(field_ref, _, out_ref, rows):
    channels, xl, yl, nz = field_ref.shape
    table = z_table(out_ref.shape[0], True)
    for c in range(channels):
        cells = field_ref[c].reshape(xl * yl, nz).astype(BF16)
        rows[pl.ds(c, 2 * KZ, stride=channels), :] = dot(table, cells, 1, 1)
    out_ref[...] = rows[...].astype(BF16).reshape(out_ref.shape)


def y_forward_kernel(modes_ref, table_ref, out_ref, rows):
    gy, size, _ = modes_ref.shape
    columns = size // 2
    straight, crossed = 0.0, 0.0
    for s in range(0, gy, 2):
        block = wide(modes_ref, s)
        straight += dot(wide(table_ref, 0, s), block, 1, 1)
        crossed += dot(wide(table_ref, 1, s), block, 1, 1)
    real = straight[:, :columns] + crossed[:, columns:]
    imag = straight[:, columns:] - crossed[:, :columns]
    for q, part in enumerate((real, imag)):
        pieces = [part[i : i + KY] for i in range(0, part.shape[0], KY)]
        spare = rows.shape[0] * LANES - out_ref.shape[2]
        pieces = jnp.concatenate([*pieces, jnp.zeros((KY, spare), F32)], axis=1)
        for i in range(rows.shape[0]):
            rows[i, pl.ds(q, KY, stride=2), :] = pieces[:, i * LANES : (i + 1) * LANES]
    joined = jnp.concatenate([rows[i] for i in range(rows.shape[0])], axis=1)
    joined = turn(joined, out_ref.shape[0], gy, False)
    out_ref[...] = joined[:, : out_ref.shape[2]].reshape(out_ref.shape).astype(BF16)


def mix_kernel(gy, modes_ref, forward_ref, weight_ref, inverse_ref, out_ref):
    xl = forward_ref.shape[0]
    columns = modes_ref.shape[2] // xl
    kz = columns // C
    gx = modes_ref.shape[0]
    cells = modes_ref[...].astype(F32).reshape(-1, modes_ref.shape[2])
    spare = jnp.zeros((2 * gx, -cells.shape[1] % LANES), F32)
    cells = turn(jnp.concatenate([cells, spare], axis=1), gx, gy, True)
    modes = jnp.zeros((columns, 2 * KX), F32)
    for x in range(xl):
        block = cells[:, x * columns : (x + 1) * columns].astype(BF16)
        modes += dot(block, forward_ref[x], 0, 0)
    turned = pltpu.roll(modes, KX, 1)
    low = lax.broadcasted_iota(jnp.int32, (C, 2 * KX), 1) < KX
    spectrum = []
    for k in range(kz):
        straight = jnp.zeros((C, 2 * KX), F32)
        crossed = jnp.zeros((C, 2 * KX), F32)
        for c in range(C):
            row = k * C + c
            weight = weight_ref[row].astype(F32)
            straight += weight * modes[row : row + 1]
            crossed += weight * turned[row : row + 1]
        real = straight - pltpu.roll(straight, KX, 1)
        imag = crossed + pltpu.roll(crossed, KX, 1)
        spectrum.append(jnp.where(low, real, imag))
    spectrum = jnp.concatenate(spectrum, axis=0).astype(BF16)
    back = [dot(inverse_ref[x], spectrum, 1, 1) for x in range(xl)]
    back = turn(jnp.concatenate([*back, spare], axis=1), gx, gy, False)
    out_ref[...] = back[:, : out_ref.shape[2]].reshape(out_ref.shape).astype(BF16)


def y_inverse_kernel(modes_ref, table_ref, out_ref, rows):
    gy, size, lanes = out_ref.shape
    columns = size // 2
    slots = range(rows.shape[0])
    whole = modes_ref[...].astype(F32).reshape(rows.shape[1], -1)
    spare = jnp.zeros((rows.shape[1], rows.shape[0] * LANES - whole.shape[1]), F32)
    padded = turn(jnp.concatenate([whole, spare], axis=1), modes_ref.shape[0], gy, True)
    for i in slots:
        rows[i] = padded[:, i * LANES : (i + 1) * LANES]
    real = jnp.concatenate([rows[i, pl.ds(0, KY, stride=2), :] for i in slots], axis=1)
    imag = jnp.concatenate([rows[i, pl.ds(1, KY, stride=2), :] for i in slots], axis=1)
    cells = []
    for i in range(0, whole.shape[1], columns):
        cells.append(jnp.concatenate([real[:, i : i + columns], imag[:, i : i + columns]], axis=1))
    cells = jnp.concatenate(cells, axis=0).astype(BF16)
    for s in range(0, gy, 2):
        straight = dot(cells, wide(table_ref, 1, s), 0, 0)
        crossed = dot(cells, wide(table_ref, 0, s), 0, 0)
        real = (straight[:columns] - crossed[columns:]).astype(BF16)
        imag = (crossed[:columns] + straight[columns:]).astype(BF16)
        for h in range(2):
            out_ref[s + h, :columns] = real[:, h * lanes : (h + 1) * lanes]
            out_ref[s + h, columns:] = imag[:, h * lanes : (h + 1) * lanes]


def output_kernel(
    modes_ref, field_ref, point_ref, bias_ref, out_ref, rows, point, result, sems
):
    channels, xl, yl, nz = field_ref.shape
    sub = 8
    size = channels * sub
    row = lax.broadcasted_iota(jnp.int32, (size, channels), 0) // sub
    col = lax.broadcasted_iota(jnp.int32, (size, channels), 1)
    pick = jnp.where(row == col, 1.0, 0.0).astype(BF16)
    tall = dot(pick, point_ref[...].astype(BF16), 1, 1).astype(BF16)
    first = lax.broadcasted_iota(jnp.int32, (size, size), 0) % sub
    second = lax.broadcasted_iota(jnp.int32, (size, size), 1) % sub
    spread = jnp.where(first == second, dot(tall, pick, 1, 1), 0.0).astype(BF16)
    for x in range(xl):
        for y in range(0, yl, sub):
            cells = field_ref[:, x, y : y + sub, :].reshape(size, nz).astype(BF16)
            point[:, x, y : y + sub, :] = dot(spread, cells, 1, 0).reshape(channels, sub, nz)
    rows[...] = modes_ref[...].reshape(rows.shape).astype(F32)
    table = z_table(modes_ref.shape[0], False)
    copies = []
    for c in range(channels):
        modes = rows[pl.ds(c, 2 * KZ, stride=channels), :].astype(BF16)
        value = point[c].reshape(xl * yl, nz) + dot(modes, table, 0, 0) + bias_ref[c]
        inner = value * (0.7978845608028654 + 0.035677408136300125 * value * value)
        half = 0.5 * value
        result[c] = (half + half * jnp.tanh(inner)).astype(BF16).reshape(xl, yl, nz)
        if c % CHUNK == CHUNK - 1:
            part = pl.ds(c + 1 - CHUNK, CHUNK)
            copies.append(
                pltpu.make_async_copy(result.at[part], out_ref.at[part], sems.at[c // CHUNK])
            )
            copies[-1].start()
    for copy in copies:
        copy.wait()


def per_device(field, spectral_weight, point_weight, point_bias):
    gx = lax.axis_size("gx")
    gy = lax.axis_size("gy")
    channels, xl, yl, nz = field.shape
    columns = KZ // gy * channels
    lanes = xl * yl
    pencil = jax.ShapeDtypeStruct((gy, 2 * columns, lanes), BF16)
    mode_rows = jax.ShapeDtypeStruct((gx, 2, xl * columns), BF16)
    small = pltpu.CompilerParams(vmem_limit_bytes=16 * MIB)

    def exchange(blocks):
        groups = rotated(gx, gy)
        return lax.all_to_all(blocks, ("gx", "gy"), 0, 0, axis_index_groups=groups, tiled=True)

    weight = spectral_weight[:, 0].transpose(1, 3, 4, 2, 0).reshape(columns, channels, 2 * KX)
    modes = pl.pallas_call(
        z_forward_kernel,
        in_specs=[vmem(), pl.BlockSpec(memory_space=pl.ANY)],
        out_specs=vmem(),
        out_shape=pencil,
        scratch_shapes=[pltpu.VMEM((2 * KZ * channels, lanes), F32)],
        compiler_params=small,
        name="z_forward",
    )(field, weight)

    modes = lax.all_to_all(modes, "gy", 0, 0, tiled=True)
    modes = pl.pallas_call(
        y_forward_kernel,
        in_specs=[vmem(), vmem()],
        out_specs=vmem(),
        out_shape=mode_rows,
        scratch_shapes=[pltpu.VMEM((pl.cdiv(xl * columns, LANES), 2 * gx, LANES), F32)],
        compiler_params=small,
        name="y_forward",
    )(modes, y_waves(gy, xl, [0, 1]))

    modes = exchange(modes)

    modes = pl.pallas_call(
        functools.partial(mix_kernel, gy),
        in_specs=[vmem(), vmem(), vmem(), vmem()],
        out_specs=vmem(),
        out_shape=mode_rows,
        compiler_params=small,
        name="mix",
    )(modes, x_pair(gx, xl, True), weight, x_pair(gx, xl, False))

    modes = exchange(modes)

    modes = pl.pallas_call(
        y_inverse_kernel,
        in_specs=[vmem(), vmem()],
        out_specs=vmem(),
        out_shape=pencil,
        scratch_shapes=[pltpu.VMEM((pl.cdiv(xl * columns, LANES), 2 * gx, LANES), F32)],
        compiler_params=small,
        name="y_inverse",
    )(modes, y_waves(gy, xl, [1, 0]))

    modes = lax.all_to_all(modes, "gy", 0, 0, tiled=True)

    return pl.pallas_call(
        output_kernel,
        in_specs=[vmem(), vmem(), vmem(), pl.BlockSpec(memory_space=pltpu.SMEM)],
        out_specs=hbm(),
        out_shape=jax.ShapeDtypeStruct(field.shape, BF16),
        scratch_shapes=[
            pltpu.VMEM((2 * KZ * channels, lanes), F32),
            pltpu.VMEM(field.shape, F32),
            pltpu.VMEM(field.shape, BF16),
            pltpu.SemaphoreType.DMA((channels // CHUNK,)),
        ],
        compiler_params=small,
        name="output",
    )(modes, field, point_weight, point_bias)


def solution(mesh):
    in_specs = (P(None, "gx", "gy", None), P(None, "gx", "gy", None, None, None), P(), P())
    out_specs = P(None, "gx", "gy", None)
    return jax.shard_map(
        per_device, mesh=mesh, in_specs=in_specs, out_specs=out_specs, check_vma=False
    )
```

```python
import functools
import math

import jax
import jax.numpy as jnp
import numpy as np
from jax import lax
from jax.experimental import pallas as pl
from jax.experimental.pallas import tpu as pltpu
from jax.sharding import PartitionSpec as P

C = 20
NX = 256
NY = 256
NZ = 256
KX = 64
KY = 64
KZ = 32
F32 = jnp.float32
BF16 = jnp.bfloat16
MIB = 1 << 20
CHUNK = 4
LANES = 128


def kept_freqs(number):
    index = np.arange(number)
    return np.where(index < number // 2, index, index - number)


def waves(first_pos, second_pos, length):
    theta = 2.0 * np.pi / length * np.mod(np.multiply.outer(first_pos, second_pos), length)
    return np.cos(theta), np.sin(theta)


def near_order(j, gy):
    return (j // 2) ^ ((gy - 2) * (j % 2)) if gy > 2 else j


def far_order(j, gx):
    n = round(gx ** (1 / 3))
    return (j % n * n + (j // n + j) % n) * n + (j // n**2 + j) % n


def z_table(gy, forward):
    shape = (2 * KZ, NZ)
    row = lax.broadcasted_iota(jnp.int32, shape, 0)
    cell = lax.broadcasted_iota(jnp.int32, shape, 1)
    own = KZ // gy
    mode = near_order(row // (2 * own), gy) * own + row % own
    imaginary = row // own % 2 == 1
    turn = jnp.where(imaginary, NZ // 4, 0)
    angle = ((mode * cell + turn) % NZ).astype(F32) * (2.0 * math.pi / NZ)
    scale = 1.0 / math.sqrt(NZ)
    if not forward:
        scale = jnp.where(mode == 0, scale, 2.0 * scale)
    return (jnp.cos(angle) * scale).astype(BF16)


def y_waves(gx, gy, xl, order):
    both = np.stack(waves(kept_freqs(KY), np.arange(NY), NY))[order] / math.sqrt(NY)
    both = both.reshape(2, KY, gy, NY // gy)
    both = both[:, far_order(np.arange(gx), gx)][:, :, near_order(np.arange(gy), gy)]
    table = np.einsum("tksy,ab->tsakby", both, np.eye(xl))
    return table.reshape(2, gy, xl * KY, xl * (NY // gy)).astype(jnp.bfloat16)


def x_pair(gx, xl, forward):
    cosine, sine = waves(kept_freqs(KX), np.arange(NX), NX)
    sign = 1.0 if forward else -1.0
    pair = np.stack([np.stack([cosine, -sign * sine]), np.stack([sign * sine, cosine])])
    if not forward:
        pair = pair.swapaxes(0, 1)
    pair = pair.reshape(2, 2, KX, gx, xl)[:, :, :, far_order(np.arange(gx), gx)] / math.sqrt(NX)
    return pair.transpose(4, 3, 0, 1, 2).reshape(xl, 2 * gx, 2 * KX).astype(jnp.bfloat16)


def dot(a, b, ca, cb):
    return lax.dot_general(a, b, (((ca,), (cb,)), ((), ())), preferred_element_type=F32)


def vmem():
    return pl.BlockSpec(memory_space=pltpu.VMEM)


def hbm():
    return pl.BlockSpec(memory_space=pltpu.HBM)


def wide(ref, *index):
    *outer, last = index
    return jnp.concatenate([ref[(*outer, last)], ref[(*outer, last + 1)]], axis=1)


def near_groups(gx, gy):
    return [[a * gy + near_order(j, gy) for j in range(gy)] for a in range(gx)]


def far_groups(gx, gy):
    step = gx // gy
    return [[far_order((j + step * g) % gx, gx) * gy + g for j in range(gx)] for g in range(gy)]


def turn(cells, gx, gy, back):
    shift = 2 * (gx // gy) * lax.axis_index("gy")
    if not back:
        shift = lax.rem(2 * gx - shift, 2 * gx)
    return pltpu.roll(cells, shift, 0)


def z_forward_kernel(field_ref, out_ref, rows):
    channels, xl, yl, nz = field_ref.shape
    table = z_table(out_ref.shape[0], True)
    for c in range(channels):
        cells = field_ref[c].reshape(xl * yl, nz).astype(BF16)
        rows[pl.ds(c, 2 * KZ, stride=channels), :] = dot(table, cells, 1, 1)
    out_ref[...] = rows[...].astype(BF16).reshape(out_ref.shape)


def y_forward_kernel(modes_ref, table_ref, out_ref, rows):
    gy, size, _ = modes_ref.shape
    columns = size // 2
    straight, crossed = 0.0, 0.0
    for s in range(0, gy, 2):
        block = wide(modes_ref, s)
        straight += dot(wide(table_ref, 0, s), block, 1, 1)
        crossed += dot(wide(table_ref, 1, s), block, 1, 1)
    real = straight[:, :columns] + crossed[:, columns:]
    imag = straight[:, columns:] - crossed[:, :columns]
    for q, part in enumerate((real, imag)):
        pieces = [part[i : i + KY] for i in range(0, part.shape[0], KY)]
        spare = rows.shape[0] * LANES - out_ref.shape[2]
        pieces = jnp.concatenate([*pieces, jnp.zeros((KY, spare), F32)], axis=1)
        for i in range(rows.shape[0]):
            rows[i, pl.ds(q, KY, stride=2), :] = pieces[:, i * LANES : (i + 1) * LANES]
    joined = jnp.concatenate([rows[i] for i in range(rows.shape[0])], axis=1)
    joined = turn(joined, out_ref.shape[0], gy, False)
    out_ref[...] = joined[:, : out_ref.shape[2]].reshape(out_ref.shape).astype(BF16)


def mix_kernel(gy, modes_ref, forward_ref, weight_ref, inverse_ref, out_ref):
    xl = forward_ref.shape[0]
    columns = modes_ref.shape[2] // xl
    kz = columns // C
    gx = modes_ref.shape[0]
    cells = modes_ref[...].astype(F32).reshape(-1, modes_ref.shape[2])
    spare = jnp.zeros((2 * gx, -cells.shape[1] % LANES), F32)
    cells = turn(jnp.concatenate([cells, spare], axis=1), gx, gy, True)
    modes = jnp.zeros((columns, 2 * KX), F32)
    for x in range(xl):
        block = cells[:, x * columns : (x + 1) * columns].astype(BF16)
        modes += dot(block, forward_ref[x], 0, 0)
    turned = pltpu.roll(modes, KX, 1)
    low = lax.broadcasted_iota(jnp.int32, (C, 2 * KX), 1) < KX
    spectrum = []
    for k in range(kz):
        straight = jnp.zeros((C, 2 * KX), F32)
        crossed = jnp.zeros((C, 2 * KX), F32)
        for c in range(C):
            row = k * C + c
            weight = weight_ref[row].astype(F32)
            straight += weight * modes[row : row + 1]
            crossed += weight * turned[row : row + 1]
        real = straight - pltpu.roll(straight, KX, 1)
        imag = crossed + pltpu.roll(crossed, KX, 1)
        spectrum.append(jnp.where(low, real, imag))
    spectrum = jnp.concatenate(spectrum, axis=0).astype(BF16)
    back = [dot(inverse_ref[x], spectrum, 1, 1) for x in range(xl)]
    back = turn(jnp.concatenate([*back, spare], axis=1), gx, gy, False)
    out_ref[...] = back[:, : out_ref.shape[2]].reshape(out_ref.shape).astype(BF16)


def y_inverse_kernel(modes_ref, table_ref, out_ref, rows):
    gy, size, lanes = out_ref.shape
    columns = size // 2
    slots = range(rows.shape[0])
    whole = modes_ref[...].astype(F32).reshape(rows.shape[1], -1)
    spare = jnp.zeros((rows.shape[1], rows.shape[0] * LANES - whole.shape[1]), F32)
    padded = turn(jnp.concatenate([whole, spare], axis=1), modes_ref.shape[0], gy, True)
    for i in slots:
        rows[i] = padded[:, i * LANES : (i + 1) * LANES]
    real = jnp.concatenate([rows[i, pl.ds(0, KY, stride=2), :] for i in slots], axis=1)
    imag = jnp.concatenate([rows[i, pl.ds(1, KY, stride=2), :] for i in slots], axis=1)
    cells = []
    for i in range(0, whole.shape[1], columns):
        cells.append(jnp.concatenate([real[:, i : i + columns], imag[:, i : i + columns]], axis=1))
    cells = jnp.concatenate(cells, axis=0).astype(BF16)
    for s in range(0, gy, 2):
        straight = dot(cells, wide(table_ref, 1, s), 0, 0)
        crossed = dot(cells, wide(table_ref, 0, s), 0, 0)
        real = (straight[:columns] - crossed[columns:]).astype(BF16)
        imag = (crossed[:columns] + straight[columns:]).astype(BF16)
        for h in range(2):
            out_ref[s + h, :columns] = real[:, h * lanes : (h + 1) * lanes]
            out_ref[s + h, columns:] = imag[:, h * lanes : (h + 1) * lanes]


def output_kernel(
    modes_ref, field_ref, point_ref, bias_ref, out_ref, rows, point, result, sems
):
    channels, xl, yl, nz = field_ref.shape
    sub = 8
    size = channels * sub
    row = lax.broadcasted_iota(jnp.int32, (size, channels), 0) // sub
    col = lax.broadcasted_iota(jnp.int32, (size, channels), 1)
    pick = jnp.where(row == col, 1.0, 0.0).astype(BF16)
    tall = dot(pick, point_ref[...].astype(BF16), 1, 1).astype(BF16)
    first = lax.broadcasted_iota(jnp.int32, (size, size), 0) % sub
    second = lax.broadcasted_iota(jnp.int32, (size, size), 1) % sub
    spread = jnp.where(first == second, dot(tall, pick, 1, 1), 0.0).astype(BF16)
    for x in range(xl):
        for y in range(0, yl, sub):
            cells = field_ref[:, x, y : y + sub, :].reshape(size, nz).astype(BF16)
            point[:, x, y : y + sub, :] = dot(spread, cells, 1, 0).reshape(channels, sub, nz)
    rows[...] = modes_ref[...].reshape(rows.shape).astype(F32)
    table = z_table(modes_ref.shape[0], False)
    copies = []
    for c in range(channels):
        modes = rows[pl.ds(c, 2 * KZ, stride=channels), :].astype(BF16)
        value = point[c].reshape(xl * yl, nz) + dot(modes, table, 0, 0) + bias_ref[c]
        inner = value * (0.7978845608028654 + 0.035677408136300125 * value * value)
        half = 0.5 * value
        result[c] = (half + half * jnp.tanh(inner)).astype(BF16).reshape(xl, yl, nz)
        if c % CHUNK == CHUNK - 1:
            part = pl.ds(c + 1 - CHUNK, CHUNK)
            copies.append(
                pltpu.make_async_copy(result.at[part], out_ref.at[part], sems.at[c // CHUNK])
            )
            copies[-1].start()
    for copy in copies:
        copy.wait()


def per_device(field, spectral_weight, point_weight, point_bias):
    gx = lax.axis_size("gx")
    gy = lax.axis_size("gy")
    channels, xl, yl, nz = field.shape
    columns = KZ // gy * channels
    lanes = xl * yl
    pencil = jax.ShapeDtypeStruct((gy, 2 * columns, lanes), BF16)
    mode_rows = jax.ShapeDtypeStruct((gx, 2, xl * columns), BF16)
    small = pltpu.CompilerParams(vmem_limit_bytes=16 * MIB)

    def exchange(blocks, groups):
        return lax.all_to_all(blocks, ("gx", "gy"), 0, 0, axis_index_groups=groups, tiled=True)

    weight = spectral_weight[:, 0].transpose(1, 3, 4, 2, 0).reshape(columns, channels, 2 * KX)
    modes = pl.pallas_call(
        z_forward_kernel,
        in_specs=[vmem()],
        out_specs=vmem(),
        out_shape=pencil,
        scratch_shapes=[pltpu.VMEM((2 * KZ * channels, lanes), F32)],
        compiler_params=small,
        name="z_forward",
    )(field)

    modes = exchange(modes, near_groups(gx, gy))
    modes = pl.pallas_call(
        y_forward_kernel,
        in_specs=[vmem(), vmem()],
        out_specs=vmem(),
        out_shape=mode_rows,
        scratch_shapes=[pltpu.VMEM((pl.cdiv(xl * columns, LANES), 2 * gx, LANES), F32)],
        compiler_params=small,
        name="y_forward",
    )(modes, y_waves(gx, gy, xl, [0, 1]))

    modes = exchange(modes, far_groups(gx, gy))

    modes = pl.pallas_call(
        functools.partial(mix_kernel, gy),
        in_specs=[vmem(), vmem(), vmem(), vmem()],
        out_specs=vmem(),
        out_shape=mode_rows,
        compiler_params=small,
        name="mix",
    )(modes, x_pair(gx, xl, True), weight, x_pair(gx, xl, False))

    modes = exchange(modes, far_groups(gx, gy))

    modes = pl.pallas_call(
        y_inverse_kernel,
        in_specs=[vmem(), vmem()],
        out_specs=vmem(),
        out_shape=pencil,
        scratch_shapes=[pltpu.VMEM((pl.cdiv(xl * columns, LANES), 2 * gx, LANES), F32)],
        compiler_params=small,
        name="y_inverse",
    )(modes, y_waves(gx, gy, xl, [1, 0]))

    modes = exchange(modes, near_groups(gx, gy))

    return pl.pallas_call(
        output_kernel,
        in_specs=[vmem(), vmem(), vmem(), pl.BlockSpec(memory_space=pltpu.SMEM)],
        out_specs=hbm(),
        out_shape=jax.ShapeDtypeStruct(field.shape, BF16),
        scratch_shapes=[
            pltpu.VMEM((2 * KZ * channels, lanes), F32),
            pltpu.VMEM(field.shape, F32),
            pltpu.VMEM(field.shape, BF16),
            pltpu.SemaphoreType.DMA((channels // CHUNK,)),
        ],
        compiler_params=small,
        name="output",
    )(modes, field, point_weight, point_bias)


def solution(mesh):
    in_specs = (P(None, "gx", "gy", None), P(None, "gx", "gy", None, None, None), P(), P())
    out_specs = P(None, "gx", "gy", None)
    return jax.shard_map(
        per_device, mesh=mesh, in_specs=in_specs, out_specs=out_specs, check_vma=False
    )
```

```python
import functools
import math

import jax
import jax.numpy as jnp
import numpy as np
from jax import lax
from jax.experimental import pallas as pl
from jax.experimental.pallas import tpu as pltpu
from jax.sharding import PartitionSpec as P

C = 20
NX = 256
NY = 256
NZ = 256
KX = 64
KY = 64
KZ = 32
F32 = jnp.float32
BF16 = jnp.bfloat16
MIB = 1 << 20
LANES = 128


def kept_freqs(number):
    index = np.arange(number)
    return np.where(index < number // 2, index, index - number)


def waves(first_pos, second_pos, length):
    theta = 2.0 * np.pi / length * np.mod(np.multiply.outer(first_pos, second_pos), length)
    return np.cos(theta), np.sin(theta)


def near_order(j, gy):
    return (j // 2) ^ ((gy - 2) * (j % 2)) if gy > 2 else j


def far_order(j, gx):
    n = round(gx ** (1 / 3))
    return (j % n * n + (j // n + j) % n) * n + (j // n**2 + j) % n


def z_table(gy, forward):
    shape = (2 * KZ, NZ)
    row = lax.broadcasted_iota(jnp.int32, shape, 0)
    cell = lax.broadcasted_iota(jnp.int32, shape, 1)
    own = KZ // gy
    mode = near_order(row // (2 * own), gy) * own + row % own
    imaginary = row // own % 2 == 1
    turn = jnp.where(imaginary, NZ // 4, 0)
    angle = ((mode * cell + turn) % NZ).astype(F32) * (2.0 * math.pi / NZ)
    scale = 1.0 / math.sqrt(NZ)
    if not forward:
        scale = jnp.where(mode == 0, scale, 2.0 * scale)
    return (jnp.cos(angle) * scale).astype(BF16)


def y_waves(gx, gy, xl, order):
    both = np.stack(waves(kept_freqs(KY), np.arange(NY), NY))[order] / math.sqrt(NY)
    both = both.reshape(2, KY, gy, NY // gy)
    both = both[:, far_order(np.arange(gx), gx)][:, :, near_order(np.arange(gy), gy)]
    table = np.einsum("tksy,ab->tsakby", both, np.eye(xl))
    return table.reshape(2, gy, xl * KY, xl * (NY // gy)).astype(jnp.bfloat16)


def x_pair(gx, xl, forward):
    cosine, sine = waves(kept_freqs(KX), np.arange(NX), NX)
    sign = 1.0 if forward else -1.0
    pair = np.stack([np.stack([cosine, -sign * sine]), np.stack([sign * sine, cosine])])
    if not forward:
        pair = pair.swapaxes(0, 1)
    pair = pair.reshape(2, 2, KX, gx, xl)[:, :, :, far_order(np.arange(gx), gx)] / math.sqrt(NX)
    return pair.transpose(4, 3, 0, 1, 2).reshape(xl, 2 * gx, 2 * KX).astype(jnp.bfloat16)


def dot(a, b, ca, cb):
    return lax.dot_general(a, b, (((ca,), (cb,)), ((), ())), preferred_element_type=F32)


def vmem():
    return pl.BlockSpec(memory_space=pltpu.VMEM)


def hbm():
    return pl.BlockSpec(memory_space=pltpu.HBM)


def wide(ref, *index):
    *outer, last = index
    return jnp.concatenate([ref[(*outer, last)], ref[(*outer, last + 1)]], axis=1)


def near_groups(gx, gy):
    return [[a * gy + near_order(j, gy) for j in range(gy)] for a in range(gx)]


def far_groups(gx, gy):
    step = gx // gy
    return [[far_order((j + step * g) % gx, gx) * gy + g for j in range(gx)] for g in range(gy)]


def turn(cells, gx, gy, back):
    shift = 2 * (gx // gy) * lax.axis_index("gy")
    if not back:
        shift = lax.rem(2 * gx - shift, 2 * gx)
    return pltpu.roll(cells, shift, 0)


def z_forward_kernel(field_ref, out_ref, rows):
    channels, xl, yl, nz = field_ref.shape
    table = z_table(out_ref.shape[0], True)
    for c in range(channels):
        cells = field_ref[c].reshape(xl * yl, nz).astype(BF16)
        rows[pl.ds(c, 2 * KZ, stride=channels), :] = dot(table, cells, 1, 1)
    out_ref[...] = rows[...].astype(BF16).reshape(out_ref.shape)


def y_forward_kernel(modes_ref, table_ref, out_ref, rows):
    gy, size, _ = modes_ref.shape
    columns = size // 2
    straight, crossed = 0.0, 0.0
    for s in range(0, gy, 2):
        block = wide(modes_ref, s)
        straight += dot(wide(table_ref, 0, s), block, 1, 1)
        crossed += dot(wide(table_ref, 1, s), block, 1, 1)
    real = straight[:, :columns] + crossed[:, columns:]
    imag = straight[:, columns:] - crossed[:, :columns]
    for q, part in enumerate((real, imag)):
        pieces = [part[i : i + KY] for i in range(0, part.shape[0], KY)]
        spare = rows.shape[0] * LANES - out_ref.shape[2]
        pieces = jnp.concatenate([*pieces, jnp.zeros((KY, spare), F32)], axis=1)
        for i in range(rows.shape[0]):
            rows[i, pl.ds(q, KY, stride=2), :] = pieces[:, i * LANES : (i + 1) * LANES]
    joined = jnp.concatenate([rows[i] for i in range(rows.shape[0])], axis=1)
    joined = turn(joined, out_ref.shape[0], gy, False)
    out_ref[...] = joined[:, : out_ref.shape[2]].reshape(out_ref.shape).astype(BF16)


def mix_kernel(gy, modes_ref, forward_ref, weight_ref, inverse_ref, _, out_ref):
    xl = forward_ref.shape[0]
    columns = modes_ref.shape[2] // xl
    kz = columns // C
    gx = modes_ref.shape[0]
    cells = modes_ref[...].astype(F32).reshape(-1, modes_ref.shape[2])
    spare = jnp.zeros((2 * gx, -cells.shape[1] % LANES), F32)
    cells = turn(jnp.concatenate([cells, spare], axis=1), gx, gy, True)
    modes = jnp.zeros((columns, 2 * KX), F32)
    for x in range(xl):
        block = cells[:, x * columns : (x + 1) * columns].astype(BF16)
        modes += dot(block, forward_ref[x], 0, 0)
    turned = pltpu.roll(modes, KX, 1)
    low = lax.broadcasted_iota(jnp.int32, (C, 2 * KX), 1) < KX
    spectrum = []
    for k in range(kz):
        straight = jnp.zeros((C, 2 * KX), F32)
        crossed = jnp.zeros((C, 2 * KX), F32)
        for c in range(C):
            row = k * C + c
            weight = weight_ref[row].astype(F32)
            straight += weight * modes[row : row + 1]
            crossed += weight * turned[row : row + 1]
        real = straight - pltpu.roll(straight, KX, 1)
        imag = crossed + pltpu.roll(crossed, KX, 1)
        spectrum.append(jnp.where(low, real, imag))
    spectrum = jnp.concatenate(spectrum, axis=0).astype(BF16)
    back = [dot(inverse_ref[x], spectrum, 1, 1) for x in range(xl)]
    back = turn(jnp.concatenate([*back, spare], axis=1), gx, gy, False)
    out_ref[...] = back[:, : out_ref.shape[2]].reshape(out_ref.shape).astype(BF16)


def y_inverse_kernel(modes_ref, table_ref, out_ref, rows):
    gy, size, lanes = out_ref.shape
    columns = size // 2
    slots = range(rows.shape[0])
    whole = modes_ref[...].astype(F32).reshape(rows.shape[1], -1)
    spare = jnp.zeros((rows.shape[1], rows.shape[0] * LANES - whole.shape[1]), F32)
    padded = turn(jnp.concatenate([whole, spare], axis=1), modes_ref.shape[0], gy, True)
    for i in slots:
        rows[i] = padded[:, i * LANES : (i + 1) * LANES]
    real = jnp.concatenate([rows[i, pl.ds(0, KY, stride=2), :] for i in slots], axis=1)
    imag = jnp.concatenate([rows[i, pl.ds(1, KY, stride=2), :] for i in slots], axis=1)
    cells = []
    for i in range(0, whole.shape[1], columns):
        cells.append(jnp.concatenate([real[:, i : i + columns], imag[:, i : i + columns]], axis=1))
    cells = jnp.concatenate(cells, axis=0).astype(BF16)
    for s in range(0, gy, 2):
        straight = dot(cells, wide(table_ref, 1, s), 0, 0)
        crossed = dot(cells, wide(table_ref, 0, s), 0, 0)
        real = (straight[:columns] - crossed[columns:]).astype(BF16)
        imag = (crossed[:columns] + straight[columns:]).astype(BF16)
        for h in range(2):
            out_ref[s + h, :columns] = real[:, h * lanes : (h + 1) * lanes]
            out_ref[s + h, columns:] = imag[:, h * lanes : (h + 1) * lanes]


def output_kernel(
    modes_ref, field_ref, point_ref, bias_ref, out_ref, rows, columns, result, sems
):
    channels, xl, yl, nz = field_ref.shape
    sub = 8
    size = channels * sub
    depth = 2 * KZ
    ones_at = depth + size
    lane = lax.broadcasted_iota(jnp.int32, (channels, 2 * LANES), 1)
    channel = lax.broadcasted_iota(jnp.int32, (channels, 2 * LANES), 0)
    spot = jnp.where((lane - depth) // sub == channel, 1.0, 0.0)
    spot = jnp.where((lane >= depth) & (lane < ones_at), spot, 0.0).astype(BF16)
    weight = dot(point_ref[...].astype(BF16), spot, 0, 0)
    bias = jnp.zeros((channels, 2 * LANES), F32)
    for c in range(channels):
        bias = jnp.where(channel == c, bias_ref[c], bias)
    high = bias.astype(BF16).astype(F32)
    weight = jnp.where(lane == ones_at, high, weight)
    weight = jnp.where(lane == ones_at + 1, bias - high, weight).astype(BF16)
    row = lax.broadcasted_iota(jnp.int32, (size, channels), 0) // sub
    col = lax.broadcasted_iota(jnp.int32, (size, channels), 1)
    pick = jnp.where(row == col, 1.0, 0.0).astype(BF16)
    first = lax.broadcasted_iota(jnp.int32, (size, 2 * LANES), 0) % sub
    second = lax.broadcasted_iota(jnp.int32, (size, 2 * LANES), 1)
    fixed = jnp.where((first == second % sub) | (second >= ones_at), dot(pick, weight, 1, 0), 0.0)
    left, right = fixed[:, :LANES], fixed[:, LANES:].astype(BF16)

    table = z_table(modes_ref.shape[0], False)
    ones = jnp.ones((2 * LANES - ones_at, nz), BF16)
    rows[...] = modes_ref[...].reshape(rows.shape).astype(F32)
    blank = jnp.zeros((xl * yl, LANES - depth), F32)
    for c in range(channels):
        modes = rows[pl.ds(c, depth, stride=channels), :]
        columns[c] = jnp.concatenate([modes.T, blank], axis=1)
    copies = []
    for x in range(xl):
        for y in range(0, yl, 2 * sub):
            halves = []
            for h in (y, y + sub):
                cells = field_ref[:, x, h : h + sub, :].reshape(size, nz).astype(BF16)
                modes = columns[:, x * yl + h : x * yl + h + sub, :].reshape(size, LANES)
                modes = jnp.concatenate([(modes + left).astype(BF16), right], axis=1)
                value = dot(modes, jnp.concatenate([table, cells, ones], axis=0), 1, 0)
                inner = value * (0.7978845608028654 + 0.035677408136300125 * value * value)
                half = 0.5 * value
                halves.append((half + half * jnp.tanh(inner)).reshape(channels, sub, nz))
            result[:, x, y : y + 2 * sub, :] = jnp.concatenate(halves, axis=1).astype(BF16)
        copies.append(pltpu.make_async_copy(result.at[:, x], out_ref.at[:, x], sems.at[x]))
        copies[-1].start()
    for copy in copies:
        copy.wait()


def per_device(field, spectral_weight, point_weight, point_bias):
    gx = lax.axis_size("gx")
    gy = lax.axis_size("gy")
    channels, xl, yl, nz = field.shape
    columns = KZ // gy * channels
    lanes = xl * yl
    pencil = jax.ShapeDtypeStruct((gy, 2 * columns, lanes), BF16)
    mode_rows = jax.ShapeDtypeStruct((gx, 2, xl * columns), BF16)
    small = pltpu.CompilerParams(vmem_limit_bytes=16 * MIB)

    def exchange(blocks, groups):
        return lax.all_to_all(blocks, ("gx", "gy"), 0, 0, axis_index_groups=groups, tiled=True)

    weight = spectral_weight[:, 0].transpose(1, 3, 4, 2, 0).reshape(columns, channels, 2 * KX)
    modes = pl.pallas_call(
        z_forward_kernel,
        in_specs=[vmem()],
        out_specs=vmem(),
        out_shape=pencil,
        scratch_shapes=[pltpu.VMEM((2 * KZ * channels, lanes), F32)],
        compiler_params=small,
        name="z_forward",
    )(field)

    modes = exchange(modes, near_groups(gx, gy))
    modes = pl.pallas_call(
        y_forward_kernel,
        in_specs=[vmem(), vmem()],
        out_specs=vmem(),
        out_shape=mode_rows,
        scratch_shapes=[pltpu.VMEM((pl.cdiv(xl * columns, LANES), 2 * gx, LANES), F32)],
        compiler_params=small,
        name="y_forward",
    )(modes, y_waves(gx, gy, xl, [0, 1]))

    modes = exchange(modes, far_groups(gx, gy))

    inverse = jnp.asarray(y_waves(gx, gy, xl, [1, 0]))
    modes = pl.pallas_call(
        functools.partial(mix_kernel, gy),
        in_specs=[vmem(), vmem(), vmem(), vmem(), pl.BlockSpec(memory_space=pl.ANY)],
        out_specs=vmem(),
        out_shape=mode_rows,
        compiler_params=small,
        name="mix",
    )(modes, x_pair(gx, xl, True), weight, x_pair(gx, xl, False), inverse)

    modes = exchange(modes, far_groups(gx, gy))

    modes = pl.pallas_call(
        y_inverse_kernel,
        in_specs=[vmem(), vmem()],
        out_specs=vmem(),
        out_shape=pencil,
        scratch_shapes=[pltpu.VMEM((pl.cdiv(xl * columns, LANES), 2 * gx, LANES), F32)],
        compiler_params=small,
        name="y_inverse",
    )(modes, inverse)

    modes = exchange(modes, near_groups(gx, gy))

    return pl.pallas_call(
        output_kernel,
        in_specs=[vmem(), vmem(), vmem(), pl.BlockSpec(memory_space=pltpu.SMEM)],
        out_specs=hbm(),
        out_shape=jax.ShapeDtypeStruct(field.shape, BF16),
        scratch_shapes=[
            pltpu.VMEM((2 * KZ * channels, lanes), F32),
            pltpu.VMEM((channels, lanes, LANES), F32),
            pltpu.VMEM(field.shape, BF16),
            pltpu.SemaphoreType.DMA((xl,)),
        ],
        compiler_params=small,
        name="output",
    )(modes, field, point_weight, point_bias)


def solution(mesh):
    in_specs = (P(None, "gx", "gy", None), P(None, "gx", "gy", None, None, None), P(), P())
    out_specs = P(None, "gx", "gy", None)
    return jax.shard_map(
        per_device, mesh=mesh, in_specs=in_specs, out_specs=out_specs, check_vma=False
    )
```

```python
import functools
import math

import jax
import jax.numpy as jnp
import numpy as np
from jax import lax
from jax.experimental import pallas as pl
from jax.experimental.pallas import tpu as pltpu
from jax.sharding import PartitionSpec as P

C = 20
NX = 256
NY = 256
NZ = 256
KX = 64
KY = 64
KZ = 32
F32 = jnp.float32
BF16 = jnp.bfloat16
MIB = 1 << 20
LANES = 128
TURN = 3


def kept_freqs(number):
    index = np.arange(number)
    return np.where(index < number // 2, index, index - number)


def waves(first_pos, second_pos, length):
    theta = 2.0 * np.pi / length * np.mod(np.multiply.outer(first_pos, second_pos), length)
    return np.cos(theta), np.sin(theta)


def near_order(j, gy):
    return (j // 2) ^ ((gy - 2) * (j % 2)) if gy > 2 else j


def far_order(j, gx):
    n = round(gx ** (1 / 3))
    return (j % n * n + (j // n + j) % n) * n + (j // n**2 + j) % n


def z_table(gy, forward):
    shape = (2 * KZ, NZ)
    row = lax.broadcasted_iota(jnp.int32, shape, 0)
    cell = lax.broadcasted_iota(jnp.int32, shape, 1)
    own = KZ // gy
    mode = near_order(row // (2 * own), gy) * own + row % own
    imaginary = row // own % 2 == 1
    turn = jnp.where(imaginary, NZ // 4, 0)
    angle = ((mode * cell + turn) % NZ).astype(F32) * (2.0 * math.pi / NZ)
    scale = 1.0 / math.sqrt(NZ)
    if not forward:
        scale = jnp.where(mode == 0, scale, 2.0 * scale)
    return (jnp.cos(angle) * scale).astype(BF16)


def y_waves(gx, gy, xl, order):
    both = np.stack(waves(kept_freqs(KY), np.arange(NY), NY))[order] / math.sqrt(NY)
    both = both.reshape(2, KY, gy, NY // gy)
    both = both[:, far_order(np.arange(gx), gx)][:, :, near_order(np.arange(gy), gy)]
    table = np.einsum("tksy,ab->tsakby", both, np.eye(xl))
    return table.reshape(2, gy, xl * KY, xl * (NY // gy)).astype(jnp.bfloat16)


def x_pair(gx, xl, forward):
    cosine, sine = waves(kept_freqs(KX), np.arange(NX), NX)
    sign = 1.0 if forward else -1.0
    pair = np.stack([np.stack([cosine, -sign * sine]), np.stack([sign * sine, cosine])])
    if not forward:
        pair = pair.swapaxes(0, 1)
    pair = pair.reshape(2, 2, KX, gx, xl)[:, :, :, far_order(np.arange(gx), gx)] / math.sqrt(NX)
    return pair.transpose(4, 3, 0, 1, 2).reshape(xl, 2 * gx, 2 * KX).astype(jnp.bfloat16)


def dot(a, b, ca, cb):
    return lax.dot_general(a, b, (((ca,), (cb,)), ((), ())), preferred_element_type=F32)


def vmem():
    return pl.BlockSpec(memory_space=pltpu.VMEM)


def hbm():
    return pl.BlockSpec(memory_space=pltpu.HBM)


def wide(ref, *index):
    *outer, last = index
    return jnp.concatenate([ref[(*outer, last)], ref[(*outer, last + 1)]], axis=1)


def near_groups(gx, gy):
    return [[a * gy + near_order(j, gy) for j in range(gy)] for a in range(gx)]


def far_groups(gx, gy):
    turns = [gx // gy * (TURN * g + 1) % gx for g in range(gy)]
    return [[far_order((j + turns[g]) % gx, gx) * gy + g for j in range(gx)] for g in range(gy)]


def turn(cells, gx, gy, back):
    shift = 2 * lax.rem(gx // gy * (TURN * lax.axis_index("gy") + 1), gx)
    if not back:
        shift = lax.rem(2 * gx - shift, 2 * gx)
    return pltpu.roll(cells, shift, 0)


def z_forward_kernel(field_ref, weight_ref, out_ref, weight_out, rows, sem):
    copy = pltpu.make_async_copy(weight_ref, weight_out, sem)
    copy.start()
    channels, xl, yl, nz = field_ref.shape
    table = z_table(out_ref.shape[0], True)
    for c in range(channels):
        cells = field_ref[c].reshape(xl * yl, nz).astype(BF16)
        rows[pl.ds(c, 2 * KZ, stride=channels), :] = dot(table, cells, 1, 1)
    out_ref[...] = rows[...].astype(BF16).reshape(out_ref.shape)
    copy.wait()


def y_forward_kernel(modes_ref, table_ref, _, out_ref, rows):
    gy, size, _ = modes_ref.shape
    columns = size // 2
    straight, crossed = 0.0, 0.0
    for s in range(0, gy, 2):
        block = wide(modes_ref, s)
        straight += dot(wide(table_ref, 0, s), block, 1, 1)
        crossed += dot(wide(table_ref, 1, s), block, 1, 1)
    real = straight[:, :columns] + crossed[:, columns:]
    imag = straight[:, columns:] - crossed[:, :columns]
    for q, part in enumerate((real, imag)):
        pieces = [part[i : i + KY] for i in range(0, part.shape[0], KY)]
        spare = rows.shape[0] * LANES - out_ref.shape[2]
        pieces = jnp.concatenate([*pieces, jnp.zeros((KY, spare), F32)], axis=1)
        for i in range(rows.shape[0]):
            rows[i, pl.ds(q, KY, stride=2), :] = pieces[:, i * LANES : (i + 1) * LANES]
    joined = jnp.concatenate([rows[i] for i in range(rows.shape[0])], axis=1)
    joined = turn(joined, out_ref.shape[0], gy, False)
    out_ref[...] = joined[:, : out_ref.shape[2]].reshape(out_ref.shape).astype(BF16)


def mix_kernel(gy, modes_ref, forward_ref, weight_ref, inverse_ref, out_ref):
    xl = forward_ref.shape[0]
    columns = modes_ref.shape[2] // xl
    kz = columns // C
    gx = modes_ref.shape[0]
    cells = modes_ref[...].astype(F32).reshape(-1, modes_ref.shape[2])
    spare = jnp.zeros((2 * gx, -cells.shape[1] % LANES), F32)
    cells = turn(jnp.concatenate([cells, spare], axis=1), gx, gy, True)
    modes = jnp.zeros((columns, 2 * KX), F32)
    for x in range(xl):
        block = cells[:, x * columns : (x + 1) * columns].astype(BF16)
        modes += dot(block, forward_ref[x], 0, 0)
    turned = pltpu.roll(modes, KX, 1)
    low = lax.broadcasted_iota(jnp.int32, (C, 2 * KX), 1) < KX
    spectrum = []
    for k in range(kz):
        straight = jnp.zeros((C, 2 * KX), F32)
        crossed = jnp.zeros((C, 2 * KX), F32)
        for c in range(C):
            row = k * C + c
            weight = weight_ref[row].astype(F32)
            straight += weight * modes[row : row + 1]
            crossed += weight * turned[row : row + 1]
        real = straight - pltpu.roll(straight, KX, 1)
        imag = crossed + pltpu.roll(crossed, KX, 1)
        spectrum.append(jnp.where(low, real, imag))
    spectrum = jnp.concatenate(spectrum, axis=0).astype(BF16)
    back = [dot(inverse_ref[x], spectrum, 1, 1) for x in range(xl)]
    back = turn(jnp.concatenate([*back, spare], axis=1), gx, gy, False)
    out_ref[...] = back[:, : out_ref.shape[2]].reshape(out_ref.shape).astype(BF16)


def y_inverse_kernel(modes_ref, table_ref, out_ref, rows):
    gy, size, lanes = out_ref.shape
    columns = size // 2
    slots = range(rows.shape[0])
    whole = modes_ref[...].astype(F32).reshape(rows.shape[1], -1)
    spare = jnp.zeros((rows.shape[1], rows.shape[0] * LANES - whole.shape[1]), F32)
    padded = turn(jnp.concatenate([whole, spare], axis=1), modes_ref.shape[0], gy, True)
    for i in slots:
        rows[i] = padded[:, i * LANES : (i + 1) * LANES]
    real = jnp.concatenate([rows[i, pl.ds(0, KY, stride=2), :] for i in slots], axis=1)
    imag = jnp.concatenate([rows[i, pl.ds(1, KY, stride=2), :] for i in slots], axis=1)
    cells = []
    for i in range(0, whole.shape[1], columns):
        cells.append(jnp.concatenate([real[:, i : i + columns], imag[:, i : i + columns]], axis=1))
    cells = jnp.concatenate(cells, axis=0).astype(BF16)
    for s in range(0, gy, 2):
        straight = dot(cells, wide(table_ref, 1, s), 0, 0)
        crossed = dot(cells, wide(table_ref, 0, s), 0, 0)
        real = (straight[:columns] - crossed[columns:]).astype(BF16)
        imag = (crossed[:columns] + straight[columns:]).astype(BF16)
        for h in range(2):
            out_ref[s + h, :columns] = real[:, h * lanes : (h + 1) * lanes]
            out_ref[s + h, columns:] = imag[:, h * lanes : (h + 1) * lanes]


def output_kernel(
    modes_ref, field_ref, point_ref, bias_ref, out_ref, rows, columns, result, sems
):
    channels, xl, yl, nz = field_ref.shape
    sub = 8
    size = channels * sub
    depth = 2 * KZ
    ones_at = depth + size
    lane = lax.broadcasted_iota(jnp.int32, (channels, 2 * LANES), 1)
    channel = lax.broadcasted_iota(jnp.int32, (channels, 2 * LANES), 0)
    spot = jnp.where((lane - depth) // sub == channel, 1.0, 0.0)
    spot = jnp.where((lane >= depth) & (lane < ones_at), spot, 0.0).astype(BF16)
    weight = dot(point_ref[...].astype(BF16), spot, 0, 0)
    bias = jnp.zeros((channels, 2 * LANES), F32)
    for c in range(channels):
        bias = jnp.where(channel == c, bias_ref[c], bias)
    high = bias.astype(BF16).astype(F32)
    weight = jnp.where(lane == ones_at, high, weight)
    weight = jnp.where(lane == ones_at + 1, bias - high, weight).astype(BF16)
    row = lax.broadcasted_iota(jnp.int32, (size, channels), 0) // sub
    col = lax.broadcasted_iota(jnp.int32, (size, channels), 1)
    pick = jnp.where(row == col, 1.0, 0.0).astype(BF16)
    first = lax.broadcasted_iota(jnp.int32, (size, 2 * LANES), 0) % sub
    second = lax.broadcasted_iota(jnp.int32, (size, 2 * LANES), 1)
    fixed = jnp.where((first == second % sub) | (second >= ones_at), dot(pick, weight, 1, 0), 0.0)
    left, right = fixed[:, :LANES], fixed[:, LANES:].astype(BF16)

    table = z_table(modes_ref.shape[0], False)
    ones = jnp.ones((2 * LANES - ones_at, nz), BF16)
    rows[...] = modes_ref[...].reshape(rows.shape).astype(F32)
    blank = jnp.zeros((xl * yl, LANES - depth), F32)
    for c in range(channels):
        modes = rows[pl.ds(c, depth, stride=channels), :]
        columns[c] = jnp.concatenate([modes.T, blank], axis=1)
    copies = []
    for x in range(xl):
        for y in range(0, yl, 2 * sub):
            halves = []
            for h in (y, y + sub):
                cells = field_ref[:, x, h : h + sub, :].reshape(size, nz).astype(BF16)
                modes = columns[:, x * yl + h : x * yl + h + sub, :].reshape(size, LANES)
                modes = jnp.concatenate([(modes + left).astype(BF16), right], axis=1)
                value = dot(modes, jnp.concatenate([table, cells, ones], axis=0), 1, 0)
                inner = value * (0.7978845608028654 + 0.035677408136300125 * value * value)
                half = 0.5 * value
                halves.append((half + half * jnp.tanh(inner)).reshape(channels, sub, nz))
            result[:, x, y : y + 2 * sub, :] = jnp.concatenate(halves, axis=1).astype(BF16)
        copies.append(pltpu.make_async_copy(result.at[:, x], out_ref.at[:, x], sems.at[x]))
        copies[-1].start()
    for copy in copies:
        copy.wait()


def per_device(field, spectral_weight, point_weight, point_bias):
    gx = lax.axis_size("gx")
    gy = lax.axis_size("gy")
    channels, xl, yl, nz = field.shape
    columns = KZ // gy * channels
    lanes = xl * yl
    pencil = jax.ShapeDtypeStruct((gy, 2 * columns, lanes), BF16)
    mode_rows = jax.ShapeDtypeStruct((gx, 2, xl * columns), BF16)
    small = pltpu.CompilerParams(vmem_limit_bytes=16 * MIB)

    def exchange(blocks, groups):
        return lax.all_to_all(blocks, ("gx", "gy"), 0, 0, axis_index_groups=groups, tiled=True)

    weight = spectral_weight[:, 0].transpose(1, 3, 4, 2, 0)
    modes, weight = pl.pallas_call(
        z_forward_kernel,
        in_specs=[vmem(), hbm()],
        out_specs=[vmem(), vmem()],
        out_shape=[pencil, jax.ShapeDtypeStruct(weight.shape, BF16)],
        scratch_shapes=[
            pltpu.VMEM((2 * KZ * channels, lanes), F32),
            pltpu.SemaphoreType.DMA,
        ],
        compiler_params=small,
        name="z_forward",
    )(field, weight)

    modes = exchange(modes, near_groups(gx, gy))
    modes, weight = lax.optimization_barrier((modes, weight))
    weight = weight.reshape(columns, channels, 2 * KX)
    modes = pl.pallas_call(
        y_forward_kernel,
        in_specs=[vmem(), vmem(), pl.BlockSpec(memory_space=pl.ANY)],
        out_specs=vmem(),
        out_shape=mode_rows,
        scratch_shapes=[pltpu.VMEM((pl.cdiv(xl * columns, LANES), 2 * gx, LANES), F32)],
        compiler_params=small,
        name="y_forward",
    )(modes, y_waves(gx, gy, xl, [0, 1]), weight)

    modes = exchange(modes, far_groups(gx, gy))

    modes = pl.pallas_call(
        functools.partial(mix_kernel, gy),
        in_specs=[vmem(), vmem(), vmem(), vmem()],
        out_specs=vmem(),
        out_shape=mode_rows,
        compiler_params=small,
        name="mix",
    )(modes, x_pair(gx, xl, True), weight, x_pair(gx, xl, False))

    modes = exchange(modes, far_groups(gx, gy))

    modes = pl.pallas_call(
        y_inverse_kernel,
        in_specs=[vmem(), vmem()],
        out_specs=vmem(),
        out_shape=pencil,
        scratch_shapes=[pltpu.VMEM((pl.cdiv(xl * columns, LANES), 2 * gx, LANES), F32)],
        compiler_params=small,
        name="y_inverse",
    )(modes, y_waves(gx, gy, xl, [1, 0]))

    modes = exchange(modes, near_groups(gx, gy))

    return pl.pallas_call(
        output_kernel,
        in_specs=[vmem(), vmem(), vmem(), pl.BlockSpec(memory_space=pltpu.SMEM)],
        out_specs=hbm(),
        out_shape=jax.ShapeDtypeStruct(field.shape, BF16),
        scratch_shapes=[
            pltpu.VMEM((2 * KZ * channels, lanes), F32),
            pltpu.VMEM((channels, lanes, LANES), F32),
            pltpu.VMEM(field.shape, BF16),
            pltpu.SemaphoreType.DMA((xl,)),
        ],
        compiler_params=small,
        name="output",
    )(modes, field, point_weight, point_bias)


def solution(mesh):
    in_specs = (P(None, "gx", "gy", None), P(None, "gx", "gy", None, None, None), P(), P())
    out_specs = P(None, "gx", "gy", None)
    return jax.shard_map(
        per_device, mesh=mesh, in_specs=in_specs, out_specs=out_specs, check_vma=False
    )
```

```python
import functools
import math

import jax
import jax.numpy as jnp
import numpy as np
from jax import lax
from jax.experimental import pallas as pl
from jax.experimental.pallas import tpu as pltpu
from jax.sharding import PartitionSpec as P

C = 20
NX = 256
NY = 256
NZ = 256
KX = 64
KY = 64
KZ = 32
F32 = jnp.float32
BF16 = jnp.bfloat16
MIB = 1 << 20
LANES = 128
TURN = 3


def kept_freqs(number):
    index = np.arange(number)
    return np.where(index < number // 2, index, index - number)


def waves(first_pos, second_pos, length):
    theta = 2.0 * np.pi / length * np.mod(np.multiply.outer(first_pos, second_pos), length)
    return np.cos(theta), np.sin(theta)


def near_order(j, gy):
    return (j // 2) ^ ((gy - 2) * (j % 2)) if gy > 2 else j


def far_order(j, gx):
    n = round(gx ** (1 / 3))
    return (j % n * n + (j // n + j) % n) * n + (j // n**2 + j) % n


def z_table(gy, forward):
    shape = (2 * KZ, NZ)
    row = lax.broadcasted_iota(jnp.int32, shape, 0)
    cell = lax.broadcasted_iota(jnp.int32, shape, 1)
    own = KZ // gy
    mode = near_order(row // (2 * own), gy) * own + row % own
    imaginary = row // own % 2 == 1
    turn = jnp.where(imaginary, NZ // 4, 0)
    angle = ((mode * cell + turn) % NZ).astype(F32) * (2.0 * math.pi / NZ)
    scale = 1.0 / math.sqrt(NZ)
    if not forward:
        scale = jnp.where(mode == 0, scale, 2.0 * scale)
    return (jnp.cos(angle) * scale).astype(BF16)


def y_waves(gx, gy, xl, order):
    both = np.stack(waves(kept_freqs(KY), np.arange(NY), NY))[order] / math.sqrt(NY)
    both = both.reshape(2, KY, gy, NY // gy)
    both = both[:, far_order(np.arange(gx), gx)][:, :, near_order(np.arange(gy), gy)]
    table = np.einsum("tksy,ab->tsakby", both, np.eye(xl))
    return table.reshape(2, gy, xl * KY, xl * (NY // gy)).astype(jnp.bfloat16)


def x_pair(gx, xl, forward):
    cosine, sine = waves(kept_freqs(KX), np.arange(NX), NX)
    sign = 1.0 if forward else -1.0
    pair = np.stack([np.stack([cosine, -sign * sine]), np.stack([sign * sine, cosine])])
    if not forward:
        pair = pair.swapaxes(0, 1)
    pair = pair.reshape(2, 2, KX, gx, xl)[:, :, :, far_order(np.arange(gx), gx)] / math.sqrt(NX)
    return pair.transpose(4, 3, 0, 1, 2).reshape(xl, 2 * gx, 2 * KX).astype(jnp.bfloat16)


def dot(a, b, ca, cb):
    return lax.dot_general(a, b, (((ca,), (cb,)), ((), ())), preferred_element_type=F32)


def vmem():
    return pl.BlockSpec(memory_space=pltpu.VMEM)


def hbm():
    return pl.BlockSpec(memory_space=pltpu.HBM)


def wide(ref, *index):
    *outer, last = index
    return jnp.concatenate([ref[(*outer, last)], ref[(*outer, last + 1)]], axis=1)


def near_groups(gx, gy):
    return [[a * gy + near_order(j, gy) for j in range(gy)] for a in range(gx)]


def far_groups(gx, gy):
    turns = [gx // gy * (TURN * g + 1) % gx for g in range(gy)]
    return [[far_order((j + turns[g]) % gx, gx) * gy + g for j in range(gx)] for g in range(gy)]


def turn(cells, gx, gy, back):
    shift = 2 * lax.rem(gx // gy * (TURN * lax.axis_index("gy") + 1), gx)
    if not back:
        shift = lax.rem(2 * gx - shift, 2 * gx)
    return pltpu.roll(cells, shift, 0)


def z_forward_kernel(field_ref, out_ref, rows):
    channels, xl, yl, nz = field_ref.shape
    table = z_table(out_ref.shape[0], True)
    for c in range(channels):
        cells = field_ref[c].reshape(xl * yl, nz).astype(BF16)
        rows[pl.ds(c, 2 * KZ, stride=channels), :] = dot(table, cells, 1, 1)
    out_ref[...] = rows[...].astype(BF16).reshape(out_ref.shape)


def y_forward_kernel(modes_ref, table_ref, out_ref, rows):
    gy, size, _ = modes_ref.shape
    columns = size // 2
    straight, crossed = 0.0, 0.0
    for s in range(0, gy, 2):
        block = wide(modes_ref, s)
        straight += dot(wide(table_ref, 0, s), block, 1, 1)
        crossed += dot(wide(table_ref, 1, s), block, 1, 1)
    real = straight[:, :columns] + crossed[:, columns:]
    imag = straight[:, columns:] - crossed[:, :columns]
    for q, part in enumerate((real, imag)):
        pieces = [part[i : i + KY] for i in range(0, part.shape[0], KY)]
        spare = rows.shape[0] * LANES - out_ref.shape[2]
        pieces = jnp.concatenate([*pieces, jnp.zeros((KY, spare), F32)], axis=1)
        for i in range(rows.shape[0]):
            rows[i, pl.ds(q, KY, stride=2), :] = pieces[:, i * LANES : (i + 1) * LANES]
    joined = jnp.concatenate([rows[i] for i in range(rows.shape[0])], axis=1)
    joined = turn(joined, out_ref.shape[0], gy, False)
    out_ref[...] = joined[:, : out_ref.shape[2]].reshape(out_ref.shape).astype(BF16)


def mix_kernel(gy, modes_ref, forward_ref, weight_ref, inverse_ref, out_ref):
    xl = forward_ref.shape[0]
    columns = modes_ref.shape[2] // xl
    kz = columns // C
    gx = modes_ref.shape[0]
    cells = modes_ref[...].astype(F32).reshape(-1, modes_ref.shape[2])
    spare = jnp.zeros((2 * gx, -cells.shape[1] % LANES), F32)
    cells = turn(jnp.concatenate([cells, spare], axis=1), gx, gy, True)
    modes = jnp.zeros((columns, 2 * KX), F32)
    for x in range(xl):
        block = cells[:, x * columns : (x + 1) * columns].astype(BF16)
        modes += dot(block, forward_ref[x], 0, 0)
    turned = pltpu.roll(modes, KX, 1)
    low = lax.broadcasted_iota(jnp.int32, (C, 2 * KX), 1) < KX
    spectrum = []
    for k in range(kz):
        straight = jnp.zeros((C, 2 * KX), F32)
        crossed = jnp.zeros((C, 2 * KX), F32)
        for c in range(C):
            row = k * C + c
            weight = weight_ref[row].astype(F32)
            straight += weight * modes[row : row + 1]
            crossed += weight * turned[row : row + 1]
        real = straight - pltpu.roll(straight, KX, 1)
        imag = crossed + pltpu.roll(crossed, KX, 1)
        spectrum.append(jnp.where(low, real, imag))
    spectrum = jnp.concatenate(spectrum, axis=0).astype(BF16)
    back = [dot(inverse_ref[x], spectrum, 1, 1) for x in range(xl)]
    back = turn(jnp.concatenate([*back, spare], axis=1), gx, gy, False)
    out_ref[...] = back[:, : out_ref.shape[2]].reshape(out_ref.shape).astype(BF16)


def y_inverse_kernel(modes_ref, table_ref, out_ref, rows):
    gy, size, lanes = out_ref.shape
    columns = size // 2
    slots = range(rows.shape[0])
    whole = modes_ref[...].astype(F32).reshape(rows.shape[1], -1)
    spare = jnp.zeros((rows.shape[1], rows.shape[0] * LANES - whole.shape[1]), F32)
    padded = turn(jnp.concatenate([whole, spare], axis=1), modes_ref.shape[0], gy, True)
    for i in slots:
        rows[i] = padded[:, i * LANES : (i + 1) * LANES]
    real = jnp.concatenate([rows[i, pl.ds(0, KY, stride=2), :] for i in slots], axis=1)
    imag = jnp.concatenate([rows[i, pl.ds(1, KY, stride=2), :] for i in slots], axis=1)
    cells = []
    for i in range(0, whole.shape[1], columns):
        cells.append(jnp.concatenate([real[:, i : i + columns], imag[:, i : i + columns]], axis=1))
    cells = jnp.concatenate(cells, axis=0).astype(BF16)
    for s in range(0, gy, 2):
        straight = dot(cells, wide(table_ref, 1, s), 0, 0)
        crossed = dot(cells, wide(table_ref, 0, s), 0, 0)
        real = (straight[:columns] - crossed[columns:]).astype(BF16)
        imag = (crossed[:columns] + straight[columns:]).astype(BF16)
        for h in range(2):
            out_ref[s + h, :columns] = real[:, h * lanes : (h + 1) * lanes]
            out_ref[s + h, columns:] = imag[:, h * lanes : (h + 1) * lanes]


def output_kernel(
    modes_ref, field_ref, point_ref, bias_ref, out_ref, rows, columns, result, sems
):
    channels, xl, yl, nz = field_ref.shape
    sub = 8
    size = channels * sub
    depth = 2 * KZ
    ones_at = depth + size
    lane = lax.broadcasted_iota(jnp.int32, (channels, 2 * LANES), 1)
    channel = lax.broadcasted_iota(jnp.int32, (channels, 2 * LANES), 0)
    spot = jnp.where((lane - depth) // sub == channel, 1.0, 0.0)
    spot = jnp.where((lane >= depth) & (lane < ones_at), spot, 0.0).astype(BF16)
    weight = dot(point_ref[...].astype(BF16), spot, 0, 0)
    bias = jnp.zeros((channels, 2 * LANES), F32)
    for c in range(channels):
        bias = jnp.where(channel == c, bias_ref[c], bias)
    high = bias.astype(BF16).astype(F32)
    weight = jnp.where(lane == ones_at, high, weight)
    weight = jnp.where(lane == ones_at + 1, bias - high, weight).astype(BF16)
    row = lax.broadcasted_iota(jnp.int32, (size, channels), 0) // sub
    col = lax.broadcasted_iota(jnp.int32, (size, channels), 1)
    pick = jnp.where(row == col, 1.0, 0.0).astype(BF16)
    first = lax.broadcasted_iota(jnp.int32, (size, 2 * LANES), 0) % sub
    second = lax.broadcasted_iota(jnp.int32, (size, 2 * LANES), 1)
    fixed = jnp.where((first == second % sub) | (second >= ones_at), dot(pick, weight, 1, 0), 0.0)
    left, right = fixed[:, :LANES], fixed[:, LANES:].astype(BF16)

    table = z_table(modes_ref.shape[0], False)
    ones = jnp.ones((2 * LANES - ones_at, nz), BF16)
    rows[...] = modes_ref[...].reshape(rows.shape).astype(F32)
    blank = jnp.zeros((xl * yl, LANES - depth), F32)
    for c in range(channels):
        modes = rows[pl.ds(c, depth, stride=channels), :]
        columns[c] = jnp.concatenate([modes.T, blank], axis=1)
    copies = []
    for x in range(xl):
        for y in range(0, yl, 2 * sub):
            halves = []
            for h in (y, y + sub):
                cells = field_ref[:, x, h : h + sub, :].reshape(size, nz).astype(BF16)
                modes = columns[:, x * yl + h : x * yl + h + sub, :].reshape(size, LANES)
                modes = jnp.concatenate([(modes + left).astype(BF16), right], axis=1)
                value = dot(modes, jnp.concatenate([table, cells, ones], axis=0), 1, 0)
                inner = value * (0.7978845608028654 + 0.035677408136300125 * value * value)
                half = 0.5 * value
                halves.append((half + half * jnp.tanh(inner)).reshape(channels, sub, nz))
            result[:, x, y : y + 2 * sub, :] = jnp.concatenate(halves, axis=1).astype(BF16)
        copies.append(pltpu.make_async_copy(result.at[:, x], out_ref.at[:, x], sems.at[x]))
        copies[-1].start()
    for copy in copies:
        copy.wait()


def per_device(field, spectral_weight, point_weight, point_bias):
    gx = lax.axis_size("gx")
    gy = lax.axis_size("gy")
    channels, xl, yl, nz = field.shape
    columns = KZ // gy * channels
    lanes = xl * yl
    pencil = jax.ShapeDtypeStruct((gy, 2 * columns, lanes), BF16)
    mode_rows = jax.ShapeDtypeStruct((gx, 2, xl * columns), BF16)
    small = pltpu.CompilerParams(vmem_limit_bytes=16 * MIB)

    def exchange(blocks, groups):
        return lax.all_to_all(blocks, ("gx", "gy"), 0, 0, axis_index_groups=groups, tiled=True)

    weight = spectral_weight[:, 0].transpose(1, 3, 4, 2, 0).reshape(columns, channels, 2 * KX)
    modes = pl.pallas_call(
        z_forward_kernel,
        in_specs=[vmem()],
        out_specs=vmem(),
        out_shape=pencil,
        scratch_shapes=[pltpu.VMEM((2 * KZ * channels, lanes), F32)],
        compiler_params=small,
        name="z_forward",
    )(field)

    modes = exchange(modes, near_groups(gx, gy))
    modes = pl.pallas_call(
        y_forward_kernel,
        in_specs=[vmem(), vmem()],
        out_specs=vmem(),
        out_shape=mode_rows,
        scratch_shapes=[pltpu.VMEM((pl.cdiv(xl * columns, LANES), 2 * gx, LANES), F32)],
        compiler_params=small,
        name="y_forward",
    )(modes, y_waves(gx, gy, xl, [0, 1]))

    modes = exchange(modes, far_groups(gx, gy))

    modes = pl.pallas_call(
        functools.partial(mix_kernel, gy),
        in_specs=[vmem(), vmem(), vmem(), vmem()],
        out_specs=vmem(),
        out_shape=mode_rows,
        compiler_params=small,
        name="mix",
    )(modes, x_pair(gx, xl, True), weight, x_pair(gx, xl, False))

    modes = exchange(modes, far_groups(gx, gy))

    modes = pl.pallas_call(
        y_inverse_kernel,
        in_specs=[vmem(), vmem()],
        out_specs=vmem(),
        out_shape=pencil,
        scratch_shapes=[pltpu.VMEM((pl.cdiv(xl * columns, LANES), 2 * gx, LANES), F32)],
        compiler_params=small,
        name="y_inverse",
    )(modes, y_waves(gx, gy, xl, [1, 0]))

    modes = exchange(modes, near_groups(gx, gy))

    return pl.pallas_call(
        output_kernel,
        in_specs=[vmem(), vmem(), vmem(), pl.BlockSpec(memory_space=pltpu.SMEM)],
        out_specs=hbm(),
        out_shape=jax.ShapeDtypeStruct(field.shape, BF16),
        scratch_shapes=[
            pltpu.VMEM((2 * KZ * channels, lanes), F32),
            pltpu.VMEM((channels, lanes, LANES), F32),
            pltpu.VMEM(field.shape, BF16),
            pltpu.SemaphoreType.DMA((xl,)),
        ],
        compiler_params=small,
        name="output",
    )(modes, field, point_weight, point_bias)


def solution(mesh):
    in_specs = (P(None, "gx", "gy", None), P(None, "gx", "gy", None, None, None), P(), P())
    out_specs = P(None, "gx", "gy", None)
    return jax.shard_map(
        per_device, mesh=mesh, in_specs=in_specs, out_specs=out_specs, check_vma=False
    )
```

```python
import functools
import math

import jax
import jax.numpy as jnp
import numpy as np
from jax import lax
from jax.experimental import pallas as pl
from jax.experimental.pallas import tpu as pltpu
from jax.sharding import PartitionSpec as P

C = 20
NX = 256
NY = 256
NZ = 256
KX = 64
KY = 64
KZ = 32
F32 = jnp.float32
BF16 = jnp.bfloat16
MIB = 1 << 20
LANES = 128
TURN = 3


def kept_freqs(number):
    index = np.arange(number)
    return np.where(index < number // 2, index, index - number)


def waves(first_pos, second_pos, length):
    theta = 2.0 * np.pi / length * np.mod(np.multiply.outer(first_pos, second_pos), length)
    return np.cos(theta), np.sin(theta)


def near_order(j, gy):
    return (j // 2) ^ ((gy - 2) * (j % 2)) if gy > 2 else j


def far_order(j, gx):
    n = round(gx ** (1 / 3))
    return (j % n * n + (j // n + j) % n) * n + (j // n**2 + j) % n


def z_table(gy, forward):
    shape = (2 * KZ, NZ)
    row = lax.broadcasted_iota(jnp.int32, shape, 0)
    cell = lax.broadcasted_iota(jnp.int32, shape, 1)
    own = KZ // gy
    mode = near_order(row // (2 * own), gy) * own + row % own
    imaginary = row // own % 2 == 1
    turn = jnp.where(imaginary, NZ // 4, 0)
    angle = ((mode * cell + turn) % NZ).astype(F32) * (2.0 * math.pi / NZ)
    scale = 1.0 / math.sqrt(NZ)
    if not forward:
        scale = jnp.where(mode == 0, scale, 2.0 * scale)
    return (jnp.cos(angle) * scale).astype(BF16)


def y_waves(gx, gy, xl, order):
    both = np.stack(waves(kept_freqs(KY), np.arange(NY), NY))[order] / math.sqrt(NY)
    both = both.reshape(2, KY, gy, NY // gy)
    both = both[:, far_order(np.arange(gx), gx)][:, :, near_order(np.arange(gy), gy)]
    table = np.einsum("tksy,ab->tsakby", both, np.eye(xl))
    return table.reshape(2, gy, xl * KY, xl * (NY // gy)).astype(jnp.bfloat16)


def x_pair(gx, xl, forward):
    cosine, sine = waves(kept_freqs(KX), np.arange(NX), NX)
    sign = 1.0 if forward else -1.0
    pair = np.stack([np.stack([cosine, -sign * sine]), np.stack([sign * sine, cosine])])
    if not forward:
        pair = pair.swapaxes(0, 1)
    pair = pair.reshape(2, 2, KX, gx, xl)[:, :, :, far_order(np.arange(gx), gx)] / math.sqrt(NX)
    return pair.transpose(4, 3, 0, 1, 2).reshape(xl, 2 * gx, 2 * KX).astype(jnp.bfloat16)


def dot(a, b, ca, cb):
    return lax.dot_general(a, b, (((ca,), (cb,)), ((), ())), preferred_element_type=F32)


def vmem():
    return pl.BlockSpec(memory_space=pltpu.VMEM)


def hbm():
    return pl.BlockSpec(memory_space=pltpu.HBM)


def wide(ref, *index):
    *outer, last = index
    return jnp.concatenate([ref[(*outer, last)], ref[(*outer, last + 1)]], axis=1)


def near_groups(gx, gy):
    return [[a * gy + near_order(j, gy) for j in range(gy)] for a in range(gx)]


def far_groups(gx, gy):
    turns = [(gx // gy + 1) * ((TURN * g + 1) % gy) % gx for g in range(gy)]
    return [[far_order((j + turns[g]) % gx, gx) * gy + g for j in range(gx)] for g in range(gy)]


def turn(cells, gx, gy, back):
    place = lax.rem(TURN * lax.axis_index("gy") + 1, gy)
    shift = 2 * lax.rem((gx // gy + 1) * place, gx)
    if not back:
        shift = lax.rem(2 * gx - shift, 2 * gx)
    return pltpu.roll(cells, shift, 0)


def z_forward_kernel(field_ref, out_ref, rows):
    channels, xl, yl, nz = field_ref.shape
    table = z_table(out_ref.shape[0], True)
    for c in range(channels):
        cells = field_ref[c].reshape(xl * yl, nz).astype(BF16)
        rows[pl.ds(c, 2 * KZ, stride=channels), :] = dot(table, cells, 1, 1)
    out_ref[...] = rows[...].astype(BF16).reshape(out_ref.shape)


def y_forward_kernel(modes_ref, table_ref, out_ref, rows):
    gy, size, _ = modes_ref.shape
    columns = size // 2
    straight, crossed = 0.0, 0.0
    for s in range(0, gy, 2):
        block = wide(modes_ref, s)
        straight += dot(wide(table_ref, 0, s), block, 1, 1)
        crossed += dot(wide(table_ref, 1, s), block, 1, 1)
    real = straight[:, :columns] + crossed[:, columns:]
    imag = straight[:, columns:] - crossed[:, :columns]
    for q, part in enumerate((real, imag)):
        pieces = [part[i : i + KY] for i in range(0, part.shape[0], KY)]
        spare = rows.shape[0] * LANES - out_ref.shape[2]
        pieces = jnp.concatenate([*pieces, jnp.zeros((KY, spare), F32)], axis=1)
        for i in range(rows.shape[0]):
            rows[i, pl.ds(q, KY, stride=2), :] = pieces[:, i * LANES : (i + 1) * LANES]
    joined = jnp.concatenate([rows[i] for i in range(rows.shape[0])], axis=1)
    joined = turn(joined, out_ref.shape[0], gy, False)
    out_ref[...] = joined[:, : out_ref.shape[2]].reshape(out_ref.shape).astype(BF16)


def mix_kernel(gy, modes_ref, forward_ref, weight_ref, inverse_ref, out_ref):
    xl = forward_ref.shape[0]
    columns = modes_ref.shape[2] // xl
    kz = columns // C
    gx = modes_ref.shape[0]
    cells = modes_ref[...].astype(F32).reshape(-1, modes_ref.shape[2])
    spare = jnp.zeros((2 * gx, -cells.shape[1] % LANES), F32)
    cells = turn(jnp.concatenate([cells, spare], axis=1), gx, gy, True)
    modes = jnp.zeros((columns, 2 * KX), F32)
    for x in range(xl):
        block = cells[:, x * columns : (x + 1) * columns].astype(BF16)
        modes += dot(block, forward_ref[x], 0, 0)
    turned = pltpu.roll(modes, KX, 1)
    low = lax.broadcasted_iota(jnp.int32, (C, 2 * KX), 1) < KX
    spectrum = []
    for k in range(kz):
        straight = jnp.zeros((C, 2 * KX), F32)
        crossed = jnp.zeros((C, 2 * KX), F32)
        for c in range(C):
            row = k * C + c
            weight = weight_ref[row].astype(F32)
            straight += weight * modes[row : row + 1]
            crossed += weight * turned[row : row + 1]
        real = straight - pltpu.roll(straight, KX, 1)
        imag = crossed + pltpu.roll(crossed, KX, 1)
        spectrum.append(jnp.where(low, real, imag))
    spectrum = jnp.concatenate(spectrum, axis=0).astype(BF16)
    back = [dot(inverse_ref[x], spectrum, 1, 1) for x in range(xl)]
    back = turn(jnp.concatenate([*back, spare], axis=1), gx, gy, False)
    out_ref[...] = back[:, : out_ref.shape[2]].reshape(out_ref.shape).astype(BF16)


def y_inverse_kernel(modes_ref, table_ref, out_ref, rows):
    gy, size, lanes = out_ref.shape
    columns = size // 2
    slots = range(rows.shape[0])
    whole = modes_ref[...].astype(F32).reshape(rows.shape[1], -1)
    spare = jnp.zeros((rows.shape[1], rows.shape[0] * LANES - whole.shape[1]), F32)
    padded = turn(jnp.concatenate([whole, spare], axis=1), modes_ref.shape[0], gy, True)
    for i in slots:
        rows[i] = padded[:, i * LANES : (i + 1) * LANES]
    real = jnp.concatenate([rows[i, pl.ds(0, KY, stride=2), :] for i in slots], axis=1)
    imag = jnp.concatenate([rows[i, pl.ds(1, KY, stride=2), :] for i in slots], axis=1)
    cells = []
    for i in range(0, whole.shape[1], columns):
        cells.append(jnp.concatenate([real[:, i : i + columns], imag[:, i : i + columns]], axis=1))
    cells = jnp.concatenate(cells, axis=0).astype(BF16)
    for s in range(0, gy, 2):
        straight = dot(cells, wide(table_ref, 1, s), 0, 0)
        crossed = dot(cells, wide(table_ref, 0, s), 0, 0)
        real = (straight[:columns] - crossed[columns:]).astype(BF16)
        imag = (crossed[:columns] + straight[columns:]).astype(BF16)
        for h in range(2):
            out_ref[s + h, :columns] = real[:, h * lanes : (h + 1) * lanes]
            out_ref[s + h, columns:] = imag[:, h * lanes : (h + 1) * lanes]


def output_kernel(
    modes_ref, field_ref, point_ref, bias_ref, out_ref, rows, columns, result, sems
):
    channels, xl, yl, nz = field_ref.shape
    sub = 8
    size = channels * sub
    depth = 2 * KZ
    ones_at = depth + size
    lane = lax.broadcasted_iota(jnp.int32, (channels, 2 * LANES), 1)
    channel = lax.broadcasted_iota(jnp.int32, (channels, 2 * LANES), 0)
    spot = jnp.where((lane - depth) // sub == channel, 1.0, 0.0)
    spot = jnp.where((lane >= depth) & (lane < ones_at), spot, 0.0).astype(BF16)
    weight = dot(point_ref[...].astype(BF16), spot, 0, 0)
    bias = jnp.zeros((channels, 2 * LANES), F32)
    for c in range(channels):
        bias = jnp.where(channel == c, bias_ref[c], bias)
    high = bias.astype(BF16).astype(F32)
    weight = jnp.where(lane == ones_at, high, weight)
    weight = jnp.where(lane == ones_at + 1, bias - high, weight).astype(BF16)
    row = lax.broadcasted_iota(jnp.int32, (size, channels), 0) // sub
    col = lax.broadcasted_iota(jnp.int32, (size, channels), 1)
    pick = jnp.where(row == col, 1.0, 0.0).astype(BF16)
    first = lax.broadcasted_iota(jnp.int32, (size, 2 * LANES), 0) % sub
    second = lax.broadcasted_iota(jnp.int32, (size, 2 * LANES), 1)
    fixed = jnp.where((first == second % sub) | (second >= ones_at), dot(pick, weight, 1, 0), 0.0)
    left, right = fixed[:, :LANES], fixed[:, LANES:].astype(BF16)

    table = z_table(modes_ref.shape[0], False)
    ones = jnp.ones((2 * LANES - ones_at, nz), BF16)
    rows[...] = modes_ref[...].reshape(rows.shape).astype(F32)
    blank = jnp.zeros((xl * yl, LANES - depth), F32)
    for c in range(channels):
        modes = rows[pl.ds(c, depth, stride=channels), :]
        columns[c] = jnp.concatenate([modes.T, blank], axis=1)
    copies = []
    for x in range(xl):
        for y in range(0, yl, 2 * sub):
            halves = []
            for h in (y, y + sub):
                cells = field_ref[:, x, h : h + sub, :].reshape(size, nz).astype(BF16)
                modes = columns[:, x * yl + h : x * yl + h + sub, :].reshape(size, LANES)
                modes = jnp.concatenate([(modes + left).astype(BF16), right], axis=1)
                value = dot(modes, jnp.concatenate([table, cells, ones], axis=0), 1, 0)
                inner = value * (0.7978845608028654 + 0.035677408136300125 * value * value)
                half = 0.5 * value
                halves.append((half + half * jnp.tanh(inner)).reshape(channels, sub, nz))
            result[:, x, y : y + 2 * sub, :] = jnp.concatenate(halves, axis=1).astype(BF16)
        copies.append(pltpu.make_async_copy(result.at[:, x], out_ref.at[:, x], sems.at[x]))
        copies[-1].start()
    for copy in copies:
        copy.wait()


def per_device(field, spectral_weight, point_weight, point_bias):
    gx = lax.axis_size("gx")
    gy = lax.axis_size("gy")
    channels, xl, yl, nz = field.shape
    columns = KZ // gy * channels
    lanes = xl * yl
    pencil = jax.ShapeDtypeStruct((gy, 2 * columns, lanes), BF16)
    mode_rows = jax.ShapeDtypeStruct((gx, 2, xl * columns), BF16)
    small = pltpu.CompilerParams(vmem_limit_bytes=16 * MIB)

    def exchange(blocks, groups):
        return lax.all_to_all(blocks, ("gx", "gy"), 0, 0, axis_index_groups=groups, tiled=True)

    weight = spectral_weight[:, 0].transpose(1, 3, 4, 2, 0).reshape(columns, channels, 2 * KX)
    modes = pl.pallas_call(
        z_forward_kernel,
        in_specs=[vmem()],
        out_specs=vmem(),
        out_shape=pencil,
        scratch_shapes=[pltpu.VMEM((2 * KZ * channels, lanes), F32)],
        compiler_params=small,
        name="z_forward",
    )(field)

    modes = exchange(modes, near_groups(gx, gy))
    modes = pl.pallas_call(
        y_forward_kernel,
        in_specs=[vmem(), vmem()],
        out_specs=vmem(),
        out_shape=mode_rows,
        scratch_shapes=[pltpu.VMEM((pl.cdiv(xl * columns, LANES), 2 * gx, LANES), F32)],
        compiler_params=small,
        name="y_forward",
    )(modes, y_waves(gx, gy, xl, [0, 1]))

    modes = exchange(modes, far_groups(gx, gy))

    modes = pl.pallas_call(
        functools.partial(mix_kernel, gy),
        in_specs=[vmem(), vmem(), vmem(), vmem()],
        out_specs=vmem(),
        out_shape=mode_rows,
        compiler_params=small,
        name="mix",
    )(modes, x_pair(gx, xl, True), weight, x_pair(gx, xl, False))

    modes = exchange(modes, far_groups(gx, gy))

    modes = pl.pallas_call(
        y_inverse_kernel,
        in_specs=[vmem(), vmem()],
        out_specs=vmem(),
        out_shape=pencil,
        scratch_shapes=[pltpu.VMEM((pl.cdiv(xl * columns, LANES), 2 * gx, LANES), F32)],
        compiler_params=small,
        name="y_inverse",
    )(modes, y_waves(gx, gy, xl, [1, 0]))

    modes = exchange(modes, near_groups(gx, gy))

    return pl.pallas_call(
        output_kernel,
        in_specs=[vmem(), vmem(), vmem(), pl.BlockSpec(memory_space=pltpu.SMEM)],
        out_specs=hbm(),
        out_shape=jax.ShapeDtypeStruct(field.shape, BF16),
        scratch_shapes=[
            pltpu.VMEM((2 * KZ * channels, lanes), F32),
            pltpu.VMEM((channels, lanes, LANES), F32),
            pltpu.VMEM(field.shape, BF16),
            pltpu.SemaphoreType.DMA((xl,)),
        ],
        compiler_params=small,
        name="output",
    )(modes, field, point_weight, point_bias)


def solution(mesh):
    in_specs = (P(None, "gx", "gy", None), P(None, "gx", "gy", None, None, None), P(), P())
    out_specs = P(None, "gx", "gy", None)
    return jax.shard_map(
        per_device, mesh=mesh, in_specs=in_specs, out_specs=out_specs, check_vma=False
    )
```

```python
import functools
import math

import jax
import jax.numpy as jnp
import numpy as np
from jax import lax
from jax.experimental import pallas as pl
from jax.experimental.pallas import tpu as pltpu
from jax.sharding import PartitionSpec as P

C = 20
NX = 256
NY = 256
NZ = 256
KX = 64
KY = 64
KZ = 32
F32 = jnp.float32
BF16 = jnp.bfloat16
MIB = 1 << 20
LANES = 128


def kept_freqs(number):
    index = np.arange(number)
    return np.where(index < number // 2, index, index - number)


def waves(first_pos, second_pos, length):
    theta = 2.0 * np.pi / length * np.mod(np.multiply.outer(first_pos, second_pos), length)
    return np.cos(theta), np.sin(theta)


def near_order(j, gy):
    return (j // 2) ^ ((gy - 2) * (j % 2)) if gy > 2 else j


def far_order(j, gx):
    n = round(gx ** (1 / 3))
    return (j % n * n + (j // n + j) % n) * n + (j // n**2 + j) % n


def z_table(gy, forward):
    shape = (2 * KZ, NZ)
    row = lax.broadcasted_iota(jnp.int32, shape, 0)
    cell = lax.broadcasted_iota(jnp.int32, shape, 1)
    own = KZ // gy
    mode = near_order(row // (2 * own), gy) * own + row % own
    imaginary = row // own % 2 == 1
    turn = jnp.where(imaginary, NZ // 4, 0)
    angle = ((mode * cell + turn) % NZ).astype(F32) * (2.0 * math.pi / NZ)
    scale = 1.0 / math.sqrt(NZ)
    if not forward:
        scale = jnp.where(mode == 0, scale, 2.0 * scale)
    return (jnp.cos(angle) * scale).astype(BF16)


def y_waves(gx, gy, xl, order):
    both = np.stack(waves(kept_freqs(KY), np.arange(NY), NY))[order] / math.sqrt(NY)
    both = both.reshape(2, KY, gy, NY // gy)
    both = both[:, far_order(np.arange(gx), gx)][:, :, near_order(np.arange(gy), gy)]
    table = np.einsum("tksy,ab->tsakby", both, np.eye(xl))
    return table.reshape(2, gy, xl * KY, xl * (NY // gy)).astype(jnp.bfloat16)


def x_pair(gx, xl, forward):
    cosine, sine = waves(kept_freqs(KX), np.arange(NX), NX)
    sign = 1.0 if forward else -1.0
    pair = np.stack([np.stack([cosine, -sign * sine]), np.stack([sign * sine, cosine])])
    if not forward:
        pair = pair.swapaxes(0, 1)
    pair = pair.reshape(2, 2, KX, gx, xl)[:, :, :, far_order(np.arange(gx), gx)] / math.sqrt(NX)
    return pair.transpose(4, 3, 0, 1, 2).reshape(xl, 2 * gx, 2 * KX).astype(jnp.bfloat16)


def dot(a, b, ca, cb):
    return lax.dot_general(a, b, (((ca,), (cb,)), ((), ())), preferred_element_type=F32)


def vmem():
    return pl.BlockSpec(memory_space=pltpu.VMEM)


def hbm():
    return pl.BlockSpec(memory_space=pltpu.HBM)


def wide(ref, *index):
    *outer, last = index
    return jnp.concatenate([ref[(*outer, last)], ref[(*outer, last + 1)]], axis=1)


def near_groups(gx, gy):
    return [[a * gy + near_order(j, gy) for j in range(gy)] for a in range(gx)]


def turns_of(g):
    return g // 2 * 16 + 8 - g % 2 * 6


def far_groups(gx, gy):
    turns = [turns_of(g) % gx for g in range(gy)]
    return [[far_order((j + turns[g]) % gx, gx) * gy + g for j in range(gx)] for g in range(gy)]


def turn(cells, gx, gy, back):
    shift = 2 * lax.rem(turns_of(lax.axis_index("gy")), gx)
    if not back:
        shift = lax.rem(2 * gx - shift, 2 * gx)
    return pltpu.roll(cells, shift, 0)


def z_forward_kernel(field_ref, out_ref, rows):
    channels, xl, yl, nz = field_ref.shape
    table = z_table(out_ref.shape[0], True)
    for c in range(channels):
        cells = field_ref[c].reshape(xl * yl, nz).astype(BF16)
        rows[pl.ds(c, 2 * KZ, stride=channels), :] = dot(table, cells, 1, 1)
    out_ref[...] = rows[...].astype(BF16).reshape(out_ref.shape)


def y_forward_kernel(modes_ref, table_ref, out_ref, rows):
    gy, size, _ = modes_ref.shape
    columns = size // 2
    straight, crossed = 0.0, 0.0
    for s in range(0, gy, 2):
        block = wide(modes_ref, s)
        straight += dot(wide(table_ref, 0, s), block, 1, 1)
        crossed += dot(wide(table_ref, 1, s), block, 1, 1)
    real = straight[:, :columns] + crossed[:, columns:]
    imag = straight[:, columns:] - crossed[:, :columns]
    for q, part in enumerate((real, imag)):
        pieces = [part[i : i + KY] for i in range(0, part.shape[0], KY)]
        spare = rows.shape[0] * LANES - out_ref.shape[2]
        pieces = jnp.concatenate([*pieces, jnp.zeros((KY, spare), F32)], axis=1)
        for i in range(rows.shape[0]):
            rows[i, pl.ds(q, KY, stride=2), :] = pieces[:, i * LANES : (i + 1) * LANES]
    joined = jnp.concatenate([rows[i] for i in range(rows.shape[0])], axis=1)
    joined = turn(joined, out_ref.shape[0], gy, False)
    out_ref[...] = joined[:, : out_ref.shape[2]].reshape(out_ref.shape).astype(BF16)


def mix_kernel(gy, modes_ref, forward_ref, weight_ref, inverse_ref, out_ref):
    xl = forward_ref.shape[0]
    columns = modes_ref.shape[2] // xl
    kz = columns // C
    gx = modes_ref.shape[0]
    cells = modes_ref[...].astype(F32).reshape(-1, modes_ref.shape[2])
    spare = jnp.zeros((2 * gx, -cells.shape[1] % LANES), F32)
    cells = turn(jnp.concatenate([cells, spare], axis=1), gx, gy, True)
    modes = jnp.zeros((columns, 2 * KX), F32)
    for x in range(xl):
        block = cells[:, x * columns : (x + 1) * columns].astype(BF16)
        modes += dot(block, forward_ref[x], 0, 0)
    turned = pltpu.roll(modes, KX, 1)
    low = lax.broadcasted_iota(jnp.int32, (C, 2 * KX), 1) < KX
    spectrum = []
    for k in range(kz):
        straight = jnp.zeros((C, 2 * KX), F32)
        crossed = jnp.zeros((C, 2 * KX), F32)
        for c in range(C):
            row = k * C + c
            weight = weight_ref[row].astype(F32)
            straight += weight * modes[row : row + 1]
            crossed += weight * turned[row : row + 1]
        real = straight - pltpu.roll(straight, KX, 1)
        imag = crossed + pltpu.roll(crossed, KX, 1)
        spectrum.append(jnp.where(low, real, imag))
    spectrum = jnp.concatenate(spectrum, axis=0).astype(BF16)
    back = [dot(inverse_ref[x], spectrum, 1, 1) for x in range(xl)]
    back = turn(jnp.concatenate([*back, spare], axis=1), gx, gy, False)
    out_ref[...] = back[:, : out_ref.shape[2]].reshape(out_ref.shape).astype(BF16)


def y_inverse_kernel(modes_ref, table_ref, out_ref, rows):
    gy, size, lanes = out_ref.shape
    columns = size // 2
    slots = range(rows.shape[0])
    whole = modes_ref[...].astype(F32).reshape(rows.shape[1], -1)
    spare = jnp.zeros((rows.shape[1], rows.shape[0] * LANES - whole.shape[1]), F32)
    padded = turn(jnp.concatenate([whole, spare], axis=1), modes_ref.shape[0], gy, True)
    for i in slots:
        rows[i] = padded[:, i * LANES : (i + 1) * LANES]
    real = jnp.concatenate([rows[i, pl.ds(0, KY, stride=2), :] for i in slots], axis=1)
    imag = jnp.concatenate([rows[i, pl.ds(1, KY, stride=2), :] for i in slots], axis=1)
    cells = []
    for i in range(0, whole.shape[1], columns):
        cells.append(jnp.concatenate([real[:, i : i + columns], imag[:, i : i + columns]], axis=1))
    cells = jnp.concatenate(cells, axis=0).astype(BF16)
    for s in range(0, gy, 2):
        straight = dot(cells, wide(table_ref, 1, s), 0, 0)
        crossed = dot(cells, wide(table_ref, 0, s), 0, 0)
        real = (straight[:columns] - crossed[columns:]).astype(BF16)
        imag = (crossed[:columns] + straight[columns:]).astype(BF16)
        for h in range(2):
            out_ref[s + h, :columns] = real[:, h * lanes : (h + 1) * lanes]
            out_ref[s + h, columns:] = imag[:, h * lanes : (h + 1) * lanes]


def output_kernel(
    modes_ref, field_ref, point_ref, bias_ref, out_ref, rows, columns, result, sems
):
    channels, xl, yl, nz = field_ref.shape
    sub = 8
    size = channels * sub
    depth = 2 * KZ
    ones_at = depth + size
    lane = lax.broadcasted_iota(jnp.int32, (channels, 2 * LANES), 1)
    channel = lax.broadcasted_iota(jnp.int32, (channels, 2 * LANES), 0)
    spot = jnp.where((lane - depth) // sub == channel, 1.0, 0.0)
    spot = jnp.where((lane >= depth) & (lane < ones_at), spot, 0.0).astype(BF16)
    weight = dot(point_ref[...].astype(BF16), spot, 0, 0)
    bias = jnp.zeros((channels, 2 * LANES), F32)
    for c in range(channels):
        bias = jnp.where(channel == c, bias_ref[c], bias)
    high = bias.astype(BF16).astype(F32)
    weight = jnp.where(lane == ones_at, high, weight)
    weight = jnp.where(lane == ones_at + 1, bias - high, weight).astype(BF16)
    row = lax.broadcasted_iota(jnp.int32, (size, channels), 0) // sub
    col = lax.broadcasted_iota(jnp.int32, (size, channels), 1)
    pick = jnp.where(row == col, 1.0, 0.0).astype(BF16)
    first = lax.broadcasted_iota(jnp.int32, (size, 2 * LANES), 0) % sub
    second = lax.broadcasted_iota(jnp.int32, (size, 2 * LANES), 1)
    fixed = jnp.where((first == second % sub) | (second >= ones_at), dot(pick, weight, 1, 0), 0.0)
    left, right = fixed[:, :LANES], fixed[:, LANES:].astype(BF16)

    table = z_table(modes_ref.shape[0], False)
    ones = jnp.ones((2 * LANES - ones_at, nz), BF16)
    rows[...] = modes_ref[...].reshape(rows.shape).astype(F32)
    blank = jnp.zeros((xl * yl, LANES - depth), F32)
    for c in range(channels):
        modes = rows[pl.ds(c, depth, stride=channels), :]
        columns[c] = jnp.concatenate([modes.T, blank], axis=1)
    copies = []
    for x in range(xl):
        for y in range(0, yl, 2 * sub):
            halves = []
            for h in (y, y + sub):
                cells = field_ref[:, x, h : h + sub, :].reshape(size, nz).astype(BF16)
                modes = columns[:, x * yl + h : x * yl + h + sub, :].reshape(size, LANES)
                modes = jnp.concatenate([(modes + left).astype(BF16), right], axis=1)
                value = dot(modes, jnp.concatenate([table, cells, ones], axis=0), 1, 0)
                inner = value * (0.7978845608028654 + 0.035677408136300125 * value * value)
                half = 0.5 * value
                halves.append((half + half * jnp.tanh(inner)).reshape(channels, sub, nz))
            result[:, x, y : y + 2 * sub, :] = jnp.concatenate(halves, axis=1).astype(BF16)
        copies.append(pltpu.make_async_copy(result.at[:, x], out_ref.at[:, x], sems.at[x]))
        copies[-1].start()
    for copy in copies:
        copy.wait()


def per_device(field, spectral_weight, point_weight, point_bias):
    gx = lax.axis_size("gx")
    gy = lax.axis_size("gy")
    channels, xl, yl, nz = field.shape
    columns = KZ // gy * channels
    lanes = xl * yl
    pencil = jax.ShapeDtypeStruct((gy, 2 * columns, lanes), BF16)
    mode_rows = jax.ShapeDtypeStruct((gx, 2, xl * columns), BF16)
    small = pltpu.CompilerParams(vmem_limit_bytes=16 * MIB)

    def exchange(blocks, groups):
        return lax.all_to_all(blocks, ("gx", "gy"), 0, 0, axis_index_groups=groups, tiled=True)

    weight = spectral_weight[:, 0].transpose(1, 3, 4, 2, 0).reshape(columns, channels, 2 * KX)
    modes = pl.pallas_call(
        z_forward_kernel,
        in_specs=[vmem()],
        out_specs=vmem(),
        out_shape=pencil,
        scratch_shapes=[pltpu.VMEM((2 * KZ * channels, lanes), F32)],
        compiler_params=small,
        name="z_forward",
    )(field)

    modes = exchange(modes, near_groups(gx, gy))
    modes = pl.pallas_call(
        y_forward_kernel,
        in_specs=[vmem(), vmem()],
        out_specs=vmem(),
        out_shape=mode_rows,
        scratch_shapes=[pltpu.VMEM((pl.cdiv(xl * columns, LANES), 2 * gx, LANES), F32)],
        compiler_params=small,
        name="y_forward",
    )(modes, y_waves(gx, gy, xl, [0, 1]))

    modes = exchange(modes, far_groups(gx, gy))

    modes = pl.pallas_call(
        functools.partial(mix_kernel, gy),
        in_specs=[vmem(), vmem(), vmem(), vmem()],
        out_specs=vmem(),
        out_shape=mode_rows,
        compiler_params=small,
        name="mix",
    )(modes, x_pair(gx, xl, True), weight, x_pair(gx, xl, False))

    modes = exchange(modes, far_groups(gx, gy))

    modes = pl.pallas_call(
        y_inverse_kernel,
        in_specs=[vmem(), vmem()],
        out_specs=vmem(),
        out_shape=pencil,
        scratch_shapes=[pltpu.VMEM((pl.cdiv(xl * columns, LANES), 2 * gx, LANES), F32)],
        compiler_params=small,
        name="y_inverse",
    )(modes, y_waves(gx, gy, xl, [1, 0]))

    modes = exchange(modes, near_groups(gx, gy))

    return pl.pallas_call(
        output_kernel,
        in_specs=[vmem(), vmem(), vmem(), pl.BlockSpec(memory_space=pltpu.SMEM)],
        out_specs=hbm(),
        out_shape=jax.ShapeDtypeStruct(field.shape, BF16),
        scratch_shapes=[
            pltpu.VMEM((2 * KZ * channels, lanes), F32),
            pltpu.VMEM((channels, lanes, LANES), F32),
            pltpu.VMEM(field.shape, BF16),
            pltpu.SemaphoreType.DMA((xl,)),
        ],
        compiler_params=small,
        name="output",
    )(modes, field, point_weight, point_bias)


def solution(mesh):
    in_specs = (P(None, "gx", "gy", None), P(None, "gx", "gy", None, None, None), P(), P())
    out_specs = P(None, "gx", "gy", None)
    return jax.shard_map(
        per_device, mesh=mesh, in_specs=in_specs, out_specs=out_specs, check_vma=False
    )
```

```python
import functools
import math

import jax
import jax.numpy as jnp
import numpy as np
from jax import lax
from jax.experimental import pallas as pl
from jax.experimental.pallas import tpu as pltpu
from jax.sharding import PartitionSpec as P

C = 20
NX = 256
NY = 256
NZ = 256
KX = 64
KY = 64
KZ = 32
F32 = jnp.float32
BF16 = jnp.bfloat16
MIB = 1 << 20
LANES = 128


def kept_freqs(number):
    index = np.arange(number)
    return np.where(index < number // 2, index, index - number)


def waves(first_pos, second_pos, length):
    theta = 2.0 * np.pi / length * np.mod(np.multiply.outer(first_pos, second_pos), length)
    return np.cos(theta), np.sin(theta)


def near_order(j, gy):
    return (j // 2) ^ ((gy - 2) * (j % 2)) if gy > 2 else j


def far_order(j, gx):
    n = round(gx ** (1 / 3))
    return (j % n * n + (j // n + j) % n) * n + (j // n**2 + j) % n


def z_table(gy, forward):
    shape = (2 * KZ, NZ)
    row = lax.broadcasted_iota(jnp.int32, shape, 0)
    cell = lax.broadcasted_iota(jnp.int32, shape, 1)
    own = KZ // gy
    mode = near_order(row // (2 * own), gy) * own + row % own
    imaginary = row // own % 2 == 1
    turn = jnp.where(imaginary, NZ // 4, 0)
    angle = ((mode * cell + turn) % NZ).astype(F32) * (2.0 * math.pi / NZ)
    scale = 1.0 / math.sqrt(NZ)
    if not forward:
        scale = jnp.where(mode == 0, scale, 2.0 * scale)
    return (jnp.cos(angle) * scale).astype(BF16)


def y_waves(gx, gy, xl, order):
    both = np.stack(waves(kept_freqs(KY), np.arange(NY), NY))[order] / math.sqrt(NY)
    both = both.reshape(2, KY, gy, NY // gy)
    both = both[:, far_order(np.arange(gx), gx)][:, :, near_order(np.arange(gy), gy)]
    table = np.einsum("tksy,ab->tsakby", both, np.eye(xl))
    return table.reshape(2, gy, xl * KY, xl * (NY // gy)).astype(jnp.bfloat16)


def x_pair(gx, xl, forward):
    cosine, sine = waves(kept_freqs(KX), np.arange(NX), NX)
    sign = 1.0 if forward else -1.0
    pair = np.stack([np.stack([cosine, -sign * sine]), np.stack([sign * sine, cosine])])
    if not forward:
        pair = pair.swapaxes(0, 1)
    pair = pair.reshape(2, 2, KX, gx, xl)[:, :, :, far_order(np.arange(gx), gx)] / math.sqrt(NX)
    return pair.transpose(4, 3, 0, 1, 2).reshape(xl, 2 * gx, 2 * KX).astype(jnp.bfloat16)


def dot(a, b, ca, cb):
    return lax.dot_general(a, b, (((ca,), (cb,)), ((), ())), preferred_element_type=F32)


def vmem():
    return pl.BlockSpec(memory_space=pltpu.VMEM)


def hbm():
    return pl.BlockSpec(memory_space=pltpu.HBM)


def wide(ref, *index):
    *outer, last = index
    return jnp.concatenate([ref[(*outer, last)], ref[(*outer, last + 1)]], axis=1)


def near_groups(gx, gy):
    return [[a * gy + near_order(j, gy) for j in range(gy)] for a in range(gx)]


def turns_of(g):
    core = g % 2
    return g // 2 * 16 + 8 - core * 6 + g // 2 % 2 * (core * 16 - 3)


def far_groups(gx, gy):
    turns = [turns_of(g) % gx for g in range(gy)]
    return [[far_order((j + turns[g]) % gx, gx) * gy + g for j in range(gx)] for g in range(gy)]


def turn(cells, gx, gy, back):
    shift = 2 * lax.rem(turns_of(lax.axis_index("gy")), gx)
    if not back:
        shift = lax.rem(2 * gx - shift, 2 * gx)
    return pltpu.roll(cells, shift, 0)


def z_forward_kernel(field_ref, out_ref, rows):
    channels, xl, yl, nz = field_ref.shape
    table = z_table(out_ref.shape[0], True)
    for c in range(channels):
        cells = field_ref[c].reshape(xl * yl, nz).astype(BF16)
        rows[pl.ds(c, 2 * KZ, stride=channels), :] = dot(table, cells, 1, 1)
    out_ref[...] = rows[...].astype(BF16).reshape(out_ref.shape)


def y_forward_kernel(modes_ref, table_ref, out_ref, rows):
    gy, size, _ = modes_ref.shape
    columns = size // 2
    straight, crossed = 0.0, 0.0
    for s in range(0, gy, 2):
        block = wide(modes_ref, s)
        straight += dot(wide(table_ref, 0, s), block, 1, 1)
        crossed += dot(wide(table_ref, 1, s), block, 1, 1)
    real = straight[:, :columns] + crossed[:, columns:]
    imag = straight[:, columns:] - crossed[:, :columns]
    for q, part in enumerate((real, imag)):
        pieces = [part[i : i + KY] for i in range(0, part.shape[0], KY)]
        spare = rows.shape[0] * LANES - out_ref.shape[2]
        pieces = jnp.concatenate([*pieces, jnp.zeros((KY, spare), F32)], axis=1)
        for i in range(rows.shape[0]):
            rows[i, pl.ds(q, KY, stride=2), :] = pieces[:, i * LANES : (i + 1) * LANES]
    joined = jnp.concatenate([rows[i] for i in range(rows.shape[0])], axis=1)
    joined = turn(joined, out_ref.shape[0], gy, False)
    out_ref[...] = joined[:, : out_ref.shape[2]].reshape(out_ref.shape).astype(BF16)


def mix_kernel(gy, modes_ref, forward_ref, weight_ref, inverse_ref, out_ref):
    xl = forward_ref.shape[0]
    columns = modes_ref.shape[2] // xl
    kz = columns // C
    gx = modes_ref.shape[0]
    cells = modes_ref[...].astype(F32).reshape(-1, modes_ref.shape[2])
    spare = jnp.zeros((2 * gx, -cells.shape[1] % LANES), F32)
    cells = turn(jnp.concatenate([cells, spare], axis=1), gx, gy, True)
    modes = jnp.zeros((columns, 2 * KX), F32)
    for x in range(xl):
        block = cells[:, x * columns : (x + 1) * columns].astype(BF16)
        modes += dot(block, forward_ref[x], 0, 0)
    turned = pltpu.roll(modes, KX, 1)
    low = lax.broadcasted_iota(jnp.int32, (C, 2 * KX), 1) < KX
    spectrum = []
    for k in range(kz):
        straight = jnp.zeros((C, 2 * KX), F32)
        crossed = jnp.zeros((C, 2 * KX), F32)
        for c in range(C):
            row = k * C + c
            weight = weight_ref[row].astype(F32)
            straight += weight * modes[row : row + 1]
            crossed += weight * turned[row : row + 1]
        real = straight - pltpu.roll(straight, KX, 1)
        imag = crossed + pltpu.roll(crossed, KX, 1)
        spectrum.append(jnp.where(low, real, imag))
    spectrum = jnp.concatenate(spectrum, axis=0).astype(BF16)
    back = [dot(inverse_ref[x], spectrum, 1, 1) for x in range(xl)]
    back = turn(jnp.concatenate([*back, spare], axis=1), gx, gy, False)
    out_ref[...] = back[:, : out_ref.shape[2]].reshape(out_ref.shape).astype(BF16)


def y_inverse_kernel(modes_ref, table_ref, out_ref, rows):
    gy, size, lanes = out_ref.shape
    columns = size // 2
    slots = range(rows.shape[0])
    whole = modes_ref[...].astype(F32).reshape(rows.shape[1], -1)
    spare = jnp.zeros((rows.shape[1], rows.shape[0] * LANES - whole.shape[1]), F32)
    padded = turn(jnp.concatenate([whole, spare], axis=1), modes_ref.shape[0], gy, True)
    for i in slots:
        rows[i] = padded[:, i * LANES : (i + 1) * LANES]
    real = jnp.concatenate([rows[i, pl.ds(0, KY, stride=2), :] for i in slots], axis=1)
    imag = jnp.concatenate([rows[i, pl.ds(1, KY, stride=2), :] for i in slots], axis=1)
    cells = []
    for i in range(0, whole.shape[1], columns):
        cells.append(jnp.concatenate([real[:, i : i + columns], imag[:, i : i + columns]], axis=1))
    cells = jnp.concatenate(cells, axis=0).astype(BF16)
    for s in range(0, gy, 2):
        straight = dot(cells, wide(table_ref, 1, s), 0, 0)
        crossed = dot(cells, wide(table_ref, 0, s), 0, 0)
        real = (straight[:columns] - crossed[columns:]).astype(BF16)
        imag = (crossed[:columns] + straight[columns:]).astype(BF16)
        for h in range(2):
            out_ref[s + h, :columns] = real[:, h * lanes : (h + 1) * lanes]
            out_ref[s + h, columns:] = imag[:, h * lanes : (h + 1) * lanes]


def output_kernel(
    modes_ref, field_ref, point_ref, bias_ref, out_ref, rows, columns, result, sems
):
    channels, xl, yl, nz = field_ref.shape
    sub = 8
    size = channels * sub
    depth = 2 * KZ
    ones_at = depth + size
    lane = lax.broadcasted_iota(jnp.int32, (channels, 2 * LANES), 1)
    channel = lax.broadcasted_iota(jnp.int32, (channels, 2 * LANES), 0)
    spot = jnp.where((lane - depth) // sub == channel, 1.0, 0.0)
    spot = jnp.where((lane >= depth) & (lane < ones_at), spot, 0.0).astype(BF16)
    weight = dot(point_ref[...].astype(BF16), spot, 0, 0)
    bias = jnp.zeros((channels, 2 * LANES), F32)
    for c in range(channels):
        bias = jnp.where(channel == c, bias_ref[c], bias)
    high = bias.astype(BF16).astype(F32)
    weight = jnp.where(lane == ones_at, high, weight)
    weight = jnp.where(lane == ones_at + 1, bias - high, weight).astype(BF16)
    row = lax.broadcasted_iota(jnp.int32, (size, channels), 0) // sub
    col = lax.broadcasted_iota(jnp.int32, (size, channels), 1)
    pick = jnp.where(row == col, 1.0, 0.0).astype(BF16)
    first = lax.broadcasted_iota(jnp.int32, (size, 2 * LANES), 0) % sub
    second = lax.broadcasted_iota(jnp.int32, (size, 2 * LANES), 1)
    fixed = jnp.where((first == second % sub) | (second >= ones_at), dot(pick, weight, 1, 0), 0.0)
    left, right = fixed[:, :LANES], fixed[:, LANES:].astype(BF16)

    table = z_table(modes_ref.shape[0], False)
    ones = jnp.ones((2 * LANES - ones_at, nz), BF16)
    rows[...] = modes_ref[...].reshape(rows.shape).astype(F32)
    blank = jnp.zeros((xl * yl, LANES - depth), F32)
    for c in range(channels):
        modes = rows[pl.ds(c, depth, stride=channels), :]
        columns[c] = jnp.concatenate([modes.T, blank], axis=1)
    copies = []
    for x in range(xl):
        for y in range(0, yl, 2 * sub):
            halves = []
            for h in (y, y + sub):
                cells = field_ref[:, x, h : h + sub, :].reshape(size, nz).astype(BF16)
                modes = columns[:, x * yl + h : x * yl + h + sub, :].reshape(size, LANES)
                modes = jnp.concatenate([(modes + left).astype(BF16), right], axis=1)
                value = dot(modes, jnp.concatenate([table, cells, ones], axis=0), 1, 0)
                inner = value * (0.7978845608028654 + 0.035677408136300125 * value * value)
                half = 0.5 * value
                halves.append((half + half * jnp.tanh(inner)).reshape(channels, sub, nz))
            result[:, x, y : y + 2 * sub, :] = jnp.concatenate(halves, axis=1).astype(BF16)
        copies.append(pltpu.make_async_copy(result.at[:, x], out_ref.at[:, x], sems.at[x]))
        copies[-1].start()
    for copy in copies:
        copy.wait()


def per_device(field, spectral_weight, point_weight, point_bias):
    gx = lax.axis_size("gx")
    gy = lax.axis_size("gy")
    channels, xl, yl, nz = field.shape
    columns = KZ // gy * channels
    lanes = xl * yl
    pencil = jax.ShapeDtypeStruct((gy, 2 * columns, lanes), BF16)
    mode_rows = jax.ShapeDtypeStruct((gx, 2, xl * columns), BF16)
    small = pltpu.CompilerParams(vmem_limit_bytes=16 * MIB)

    def exchange(blocks, groups):
        return lax.all_to_all(blocks, ("gx", "gy"), 0, 0, axis_index_groups=groups, tiled=True)

    weight = spectral_weight[:, 0].transpose(1, 3, 4, 2, 0).reshape(columns, channels, 2 * KX)
    modes = pl.pallas_call(
        z_forward_kernel,
        in_specs=[vmem()],
        out_specs=vmem(),
        out_shape=pencil,
        scratch_shapes=[pltpu.VMEM((2 * KZ * channels, lanes), F32)],
        compiler_params=small,
        name="z_forward",
    )(field)

    modes = exchange(modes, near_groups(gx, gy))
    modes = pl.pallas_call(
        y_forward_kernel,
        in_specs=[vmem(), vmem()],
        out_specs=vmem(),
        out_shape=mode_rows,
        scratch_shapes=[pltpu.VMEM((pl.cdiv(xl * columns, LANES), 2 * gx, LANES), F32)],
        compiler_params=small,
        name="y_forward",
    )(modes, y_waves(gx, gy, xl, [0, 1]))

    modes = exchange(modes, far_groups(gx, gy))

    modes = pl.pallas_call(
        functools.partial(mix_kernel, gy),
        in_specs=[vmem(), vmem(), vmem(), vmem()],
        out_specs=vmem(),
        out_shape=mode_rows,
        compiler_params=small,
        name="mix",
    )(modes, x_pair(gx, xl, True), weight, x_pair(gx, xl, False))

    modes = exchange(modes, far_groups(gx, gy))

    modes = pl.pallas_call(
        y_inverse_kernel,
        in_specs=[vmem(), vmem()],
        out_specs=vmem(),
        out_shape=pencil,
        scratch_shapes=[pltpu.VMEM((pl.cdiv(xl * columns, LANES), 2 * gx, LANES), F32)],
        compiler_params=small,
        name="y_inverse",
    )(modes, y_waves(gx, gy, xl, [1, 0]))

    modes = exchange(modes, near_groups(gx, gy))

    return pl.pallas_call(
        output_kernel,
        in_specs=[vmem(), vmem(), vmem(), pl.BlockSpec(memory_space=pltpu.SMEM)],
        out_specs=hbm(),
        out_shape=jax.ShapeDtypeStruct(field.shape, BF16),
        scratch_shapes=[
            pltpu.VMEM((2 * KZ * channels, lanes), F32),
            pltpu.VMEM((channels, lanes, LANES), F32),
            pltpu.VMEM(field.shape, BF16),
            pltpu.SemaphoreType.DMA((xl,)),
        ],
        compiler_params=small,
        name="output",
    )(modes, field, point_weight, point_bias)


def solution(mesh):
    in_specs = (P(None, "gx", "gy", None), P(None, "gx", "gy", None, None, None), P(), P())
    out_specs = P(None, "gx", "gy", None)
    return jax.shard_map(
        per_device, mesh=mesh, in_specs=in_specs, out_specs=out_specs, check_vma=False
    )
```
